32 devices in a mesh: sec: 16 (over z, y, x), tile: 2 (over core).
Axes of the slice: x: 2, y: 2, z: 4, core: 2. Of those that a mesh axis runs over, the one named last changes fastest.
Arguments:
- sections: bfloat16 [16, 256, 4096], P('sec', None, 'tile'), may hold values from -120 to 120, as said below
- calibration_knots: int32 [17], replicated, may hold values from 200 to 8200, as said below
- target_offset: int32 [4, 64], P(None, 'tile'), may hold values from 0 to 63
- target_step: int32 [4, 64], P(None, 'tile'), may hold values from 32 to 63
Outputs:
- resampled: bfloat16 [16, 256, 4096], P(None, 'sec', 'tile')
The draws below stay inside these ranges and needn't reach their ends.
Inputs may be any that keep to these rules, and one draw needn't show every extreme that they name: sections are intensities correlated from section to section. calibration_knots fall strictly from the first knot, 8200, to the last, 200.
All inputs are finite; a program needn't handle non-finite values.
Results may differ from the reference program's by a relative error of at most 0.0044.
Values may be sent and summed in bfloat16 or wider, within the bound.
No kernel may reach another device: no remote copies, remote signals or barrier semaphores. Data moves between devices by JAX's collectives and lax.ppermute only.
A program may use at most 256 MiB of HBM per device.

```python
import jax
import jax.numpy as jnp
from jax import lax

COLS = 4096
TILE = 64
AHEAD = 4
KNOTS = 17
ROWS = 256
NSEC = 16
NOUT = 16
TR = 4
TC = 64


def draw_sections(key, part):
    key_base, key_jitter, key_noise = jax.random.split(key, 3)
    tile_rows = ROWS // TILE
    tile_cols = COLS // TILE
    baseline = jax.random.uniform(key_base, (tile_rows, tile_cols), jnp.float32, 0.35, 0.95)
    jitter = jax.random.uniform(key_jitter, (NSEC, tile_rows, tile_cols), jnp.float32, 0.6, 1.0)
    factors = baseline[None] * jitter
    tile_scale = jnp.ones((tile_rows, tile_cols), jnp.float32)
    tile_shift = jnp.zeros((tile_rows, tile_cols), jnp.float32)
    scale_pixels = jnp.repeat(jnp.repeat(tile_scale, TILE, 0), TILE, 1)
    shift_pixels = jnp.repeat(jnp.repeat(tile_shift, TILE, 0), TILE, 1)
    layer_keys = jax.random.split(key_noise, NSEC)

    def advance(previous, layer):
        factor_tile, layer_key = layer
        spread = jnp.repeat(jnp.repeat(factor_tile, TILE, 0), TILE, 1)
        noise = jnp.clip(jax.random.normal(layer_key, (ROWS, COLS), jnp.float32), -6.0, 6.0)
        current = spread * previous + jnp.sqrt(1.0 - spread * spread) * noise
        drawn = current * scale_pixels + shift_pixels
        return (current, drawn.astype(jnp.bfloat16))
    start = jnp.zeros((ROWS, COLS), jnp.float32)
    finished, stacked = lax.scan(advance, start, (factors, layer_keys))
    return stacked


def draw_calibration_knots(key, part):
    key_steps = jax.random.fold_in(key, 11)
    increments = jax.random.randint(key_steps, (KNOTS - 1,), 10, 1000, jnp.int32)
    tail_sums = jnp.cumsum(increments[::-1])[::-1].astype(jnp.int32)
    scaled = tail_sums * 8000 // tail_sums[0]
    knots = jnp.concatenate([scaled, jnp.zeros((1,), jnp.int32)]) + 200
    return knots.astype(jnp.int32)


def touch_ends(array, rng, low, largest):
    longest = array.shape.index(max(array.shape))
    spots = []
    for shift in (0, 1):
        where = [jax.random.randint(jax.random.fold_in(rng, axis), (), 0, length) for axis, length in enumerate(array.shape)]
        where[longest] = (where[longest] + shift) % array.shape[longest]
        spots.append(tuple(where))
    return array.at[spots[0]].set(low).at[spots[1]].set(largest)


def setup_inputs(seed: int = 0) -> dict:
    arg_keys = jax.random.split(jax.random.key(seed), 5)
    return {
        "sections": draw_sections(jax.random.fold_in(arg_keys[4], 71), 0),
        "calibration_knots": draw_calibration_knots(jax.random.fold_in(arg_keys[4], 71), 0),
        "target_offset": touch_ends(jax.random.randint(arg_keys[2], (TR, TC), 0, 64), jax.random.fold_in(arg_keys[2], 1), 0, 63).astype(jnp.int32),
        "target_step": touch_ends(jax.random.randint(arg_keys[3], (TR, TC), 32, 64), jax.random.fold_in(arg_keys[3], 1), 32, 63).astype(jnp.int32),
    }


epsilon = 1e-06

def shrink(pixels):
    leading = pixels.shape[:-2]
    row_total = pixels.shape[-2]
    col_total = pixels.shape[-1]
    blocks = pixels.astype(jnp.float32).reshape(leading + (row_total // 2, 2, col_total // 2, 2))
    return lax.optimization_barrier(jnp.mean(blocks, axis=(-3, -1))).astype(jnp.bfloat16)

def moments(current, following, row_group, half_tile):
    leading = current.shape[:-2]
    tiled_shape = leading + (current.shape[-2] // row_group, row_group, current.shape[-1] // half_tile, half_tile)
    first_tile = current.astype(jnp.float32).reshape(tiled_shape)
    second_tile = following.astype(jnp.float32).reshape(tiled_shape)

    def tile_total(values):
        return lax.optimization_barrier(jnp.sum(values, axis=(-3, -1)))
    return (tile_total(first_tile), tile_total(second_tile), tile_total(first_tile * first_tile), tile_total(second_tile * second_tile), tile_total(first_tile * second_tile))

def correlate(moment_sums, samples):
    sum_first, sum_second, sum_ff, sum_ss, sum_fs = moment_sums
    mean_first = sum_first / samples
    mean_second = sum_second / samples
    covariance = sum_fs / samples - mean_first * mean_second
    var_first = sum_ff / samples - mean_first * mean_first
    var_second = sum_ss / samples - mean_second * mean_second
    return covariance / jnp.sqrt(var_first * var_second + epsilon)

def calibrate(correlation, knot_values):
    knot_total = knot_values.shape[0]
    knot_grid = -1.0 + jnp.arange(knot_total, dtype=jnp.float32) * (2.0 / (knot_total - 1))
    hat_weights = jnp.maximum(0.0, 1.0 - jnp.abs(correlation[..., None] - knot_grid) * ((knot_total - 1) / 2.0))
    return lax.optimization_barrier(jnp.sum(hat_weights * (knot_values.astype(jnp.float32) / 1000.0), axis=-1))

def exclusive_last(values):
    running = jnp.cumsum(values, axis=-1)
    return jnp.concatenate([jnp.zeros(values.shape[:-1] + (1,), jnp.float32), running[..., :-1]], axis=-1)

def resample_weights(depths, offsets, strides, outputs):
    section_total = depths.shape[-1]
    grid_index = jnp.arange(outputs, dtype=jnp.int32)
    fraction = (offsets[..., None] + grid_index * strides[..., None]).astype(jnp.float32) / (64.0 * outputs)
    target = depths[..., -1:] * fraction
    bracket = lax.optimization_barrier(jnp.sum((depths[..., None, 1:] <= target[..., None]).astype(jnp.int32), axis=-1))
    bracket = jnp.minimum(bracket, section_total - 2)
    section_places = jnp.arange(section_total, dtype=jnp.int32)
    lower_depth = lax.optimization_barrier(jnp.sum(jnp.where(section_places == bracket[..., None], depths[..., None, :], 0.0), axis=-1))
    upper_depth = lax.optimization_barrier(jnp.sum(jnp.where(section_places == bracket[..., None] + 1, depths[..., None, :], 0.0), axis=-1))
    lifted = bracket.astype(jnp.float32) + (target - lower_depth) / (upper_depth - lower_depth)
    spread = jnp.abs(lifted[..., None] - section_places.astype(jnp.float32))
    return jnp.maximum(0.0, 1.0 - spread).astype(jnp.bfloat16)

def reference(sections, calibration_knots, target_offset, target_step):
    section_total = sections.shape[0]
    half_tile = TILE // 2
    reduced = shrink(sections)
    numerator = jnp.zeros((section_total, ROWS // TILE, COLS // TILE), jnp.float32)
    denominator = jnp.zeros((section_total, 1, 1), jnp.float32)
    for spacing in range(1, AHEAD + 1):
        forward = jnp.concatenate([reduced[spacing:], jnp.zeros((spacing,) + reduced.shape[1:], jnp.bfloat16)], axis=0)
        correlation = correlate(moments(reduced, forward, half_tile, half_tile), float(half_tile * half_tile))
        usable = (jnp.arange(section_total, dtype=jnp.int32) + spacing < section_total).astype(jnp.float32)[:, None, None]
        numerator = numerator + usable * (spacing * calibrate(correlation, calibration_knots))
        denominator = denominator + usable * float(spacing * spacing)
    thickness = numerator / jnp.maximum(denominator, 1.0)
    depths = exclusive_last(jnp.moveaxis(thickness, 0, -1))
    weights = resample_weights(depths, target_offset, target_step, NOUT)

    def one_row(inputs):
        weights_row, tile_row = inputs
        slab_pixels = lax.dynamic_slice_in_dim(sections, tile_row * TILE, TILE, 1)
        slab_pixels = slab_pixels.astype(jnp.float32).reshape(section_total, TILE, COLS // TILE, TILE)
        mixed_rows = jnp.einsum('tjs,srtc->jrtc', weights_row.astype(jnp.float32), slab_pixels, precision=lax.Precision.HIGHEST)
        return mixed_rows.reshape(NOUT, TILE, COLS).astype(jnp.bfloat16)
    per_row = lax.map(one_row, (weights, jnp.arange(ROWS // TILE, dtype=jnp.int32)))
    return jnp.transpose(per_row, (1, 0, 2, 3)).reshape(NOUT, ROWS, COLS)
```

```python
import functools

import jax
import jax.numpy as jnp
from jax import lax
from jax.experimental import pallas as pl
from jax.experimental.pallas import tpu as pltpu
from jax.sharding import PartitionSpec as P

TILE = 64
AHEAD = 4
LANES = 128
EPSILON = 1e-06


def from_behind(value, axis, steps):
    count = lax.axis_size(axis)
    first, last = (max(0, -steps), min(count, count - steps))
    return lax.ppermute(value, axis, [(source, source + steps) for source in range(first, last)])


def shrink(pixels):
    leading = pixels.shape[:-2]
    row_total = pixels.shape[-2]
    col_total = pixels.shape[-1]
    blocks = pixels.astype(jnp.float32).reshape(leading + (row_total // 2, 2, col_total // 2, 2))
    return jnp.mean(blocks, axis=(-3, -1)).astype(jnp.bfloat16)


def moments(current, following, row_group, half_tile):
    leading = current.shape[:-2]
    tiled_shape = leading + (
        current.shape[-2] // row_group,
        row_group,
        current.shape[-1] // half_tile,
        half_tile,
    )
    first_tile = current.astype(jnp.float32).reshape(tiled_shape)
    second_tile = following.astype(jnp.float32).reshape(tiled_shape)

    def tile_total(values):
        return jnp.sum(values, axis=(-3, -1))

    return (
        tile_total(first_tile),
        tile_total(second_tile),
        tile_total(first_tile * first_tile),
        tile_total(second_tile * second_tile),
        tile_total(first_tile * second_tile),
    )


def correlate(moment_sums, samples):
    sum_first, sum_second, sum_ff, sum_ss, sum_fs = moment_sums
    mean_first = sum_first / samples
    mean_second = sum_second / samples
    covariance = sum_fs / samples - mean_first * mean_second
    var_first = sum_ff / samples - mean_first * mean_first
    var_second = sum_ss / samples - mean_second * mean_second
    return covariance / jnp.sqrt(var_first * var_second + EPSILON)


def calibrate(correlation, knot_values):
    knot_total = knot_values.shape[0]
    knot_grid = -1.0 + jnp.arange(knot_total, dtype=jnp.float32) * (2.0 / (knot_total - 1))
    hat_weights = jnp.maximum(
        0.0, 1.0 - jnp.abs(correlation[..., None] - knot_grid) * ((knot_total - 1) / 2.0)
    )
    return jnp.sum(hat_weights * (knot_values.astype(jnp.float32) / 1000.0), axis=-1)


def exclusive_last(values):
    running = jnp.cumsum(values, axis=-1)
    return jnp.concatenate(
        [jnp.zeros(values.shape[:-1] + (1,), jnp.float32), running[..., :-1]], axis=-1
    )


def resample_weights(depths, offsets, strides, outputs):
    section_total = depths.shape[-1]
    grid_index = jnp.arange(outputs, dtype=jnp.int32)
    fraction = (offsets[..., None] + grid_index * strides[..., None]).astype(jnp.float32) / (
        64.0 * outputs
    )
    target = depths[..., -1:] * fraction
    bracket = jnp.sum((depths[..., None, 1:] <= target[..., None]).astype(jnp.int32), axis=-1)
    bracket = jnp.minimum(bracket, section_total - 2)
    section_places = jnp.arange(section_total, dtype=jnp.int32)
    lower_depth = jnp.sum(
        jnp.where(section_places == bracket[..., None], depths[..., None, :], 0.0), axis=-1
    )
    upper_depth = jnp.sum(
        jnp.where(section_places == bracket[..., None] + 1, depths[..., None, :], 0.0), axis=-1
    )
    lifted = bracket.astype(jnp.float32) + (target - lower_depth) / (upper_depth - lower_depth)
    spread = jnp.abs(lifted[..., None] - section_places.astype(jnp.float32))
    return jnp.maximum(0.0, 1.0 - spread).astype(jnp.bfloat16)


def plain_per_device(sections, calibration_knots, target_offset, target_step):
    section_total = lax.axis_size("sec")
    position = lax.axis_index("sec")
    half_tile = TILE // 2
    samples = float(half_tile * half_tile)
    row_total = sections.shape[1]
    rows_local = row_total // section_total
    tile_rows = row_total // TILE
    tiles_wide = sections.shape[2] // TILE
    tile_row = position * rows_local // TILE
    pencils = lax.all_to_all(sections, "sec", split_axis=1, concat_axis=0, tiled=True)
    reduced = shrink(sections[0])
    numerator = jnp.zeros((tile_rows, tiles_wide), jnp.float32)
    denominator = jnp.zeros((), jnp.float32)
    for spacing in range(1, AHEAD + 1):
        forward = from_behind(reduced, "sec", -spacing)
        correlation = correlate(moments(reduced, forward, half_tile, half_tile), samples)
        usable = (position + spacing < section_total).astype(jnp.float32)
        numerator = numerator + usable * (spacing * calibrate(correlation, calibration_knots))
        denominator = denominator + usable * float(spacing * spacing)
    thickness = numerator / jnp.maximum(denominator, 1.0)
    spread_rows = jnp.repeat(thickness, TILE, axis=0)[None]
    carried_maps = lax.all_to_all(spread_rows, "sec", split_axis=1, concat_axis=0, tiled=True)
    column_maps = jnp.transpose(carried_maps[:, 0, :])
    depths = exclusive_last(column_maps)
    offsets_row = lax.dynamic_index_in_dim(target_offset, tile_row, 0, keepdims=False)
    strides_row = lax.dynamic_index_in_dim(target_step, tile_row, 0, keepdims=False)
    weights = resample_weights(depths, offsets_row, strides_row, section_total)
    pencil_tiles = pencils.reshape(section_total, rows_local, tiles_wide, TILE)
    resampled = jnp.einsum(
        "tjs,srtc->jrtc", weights, pencil_tiles, preferred_element_type=jnp.float32
    )
    return resampled.reshape(section_total, rows_local, sections.shape[2]).astype(jnp.bfloat16)


def one_hot(shape, row_of, col_of):
    rows = lax.broadcasted_iota(jnp.int32, shape, 0)
    cols = lax.broadcasted_iota(jnp.int32, shape, 1)
    return (row_of(rows) == col_of(cols)).astype(jnp.float32).astype(jnp.bfloat16)


def shift_up(values, steps):
    if steps == 0:
        return values
    return jnp.concatenate([values[steps:], jnp.zeros_like(values[:steps])], axis=0)


def split_dot(values, ones):
    high = values.astype(jnp.bfloat16)
    rest = values - high.astype(jnp.float32)
    middle = rest.astype(jnp.bfloat16)
    low = (rest - middle.astype(jnp.float32)).astype(jnp.bfloat16)
    dot = functools.partial(jnp.dot, preferred_element_type=jnp.float32)
    return dot(high, ones) + (dot(middle, ones) + dot(low, ones))


def sums_kernel(x_ref, sums_ref, pairs_ref, totals_ref):
    sections, rows, cols = x_ref.shape
    half = cols // 2
    tiles = cols // TILE
    pairing = one_hot((2 * LANES, LANES), lambda r: r // 2, lambda c: c)
    for g in range(half // LANES):
        wide = x_ref[:, :, 2 * LANES * g : 2 * LANES * (g + 1)]
        pairs_ref[g] = jnp.dot(
            wide.reshape(sections * rows, 2 * LANES),
            pairing,
            preferred_element_type=jnp.float32,
        )
    for g in range(half // LANES):
        lanes = pl.ds(LANES * g, LANES)
        totals = [jnp.zeros((sections, LANES), jnp.float32)] * (AHEAD + 2)
        for r in range(rows // 2):
            upper = pairs_ref[g, pl.ds(2 * r, sections, stride=rows), :]
            lower = pairs_ref[g, pl.ds(2 * r + 1, sections, stride=rows), :]
            reduced = ((upper + lower) * 0.25).astype(jnp.bfloat16).astype(jnp.float32)
            totals[0] = totals[0] + reduced
            for k in range(AHEAD + 1):
                totals[k + 1] = totals[k + 1] + reduced * shift_up(reduced, k)
        for q in range(AHEAD + 2):
            totals_ref[sections * q : sections * (q + 1), lanes] = totals[q]
    of_tile = one_hot((half, tiles), lambda r: r // (TILE // 2), lambda c: c)
    sums = split_dot(totals_ref[...], of_tile)
    wide = LANES // tiles
    height = sums.shape[0] // wide
    for q in range(wide):
        sums_ref[:, tiles * q : tiles * (q + 1)] = sums[height * q : height * (q + 1)]


def resample_kernel(
    tile_row_ref, knots_ref, offset_ref, step_ref, *refs
):
    *sums_refs, x_ref, out_ref, weights_ref, spread_ref = refs
    sections, rows, cols = x_ref.shape
    outputs = out_ref.shape[0]
    tiles = cols // TILE
    samples = float((TILE // 2) ** 2)
    packed = sums_refs[0][...]
    for ref in sums_refs[1:]:
        packed = packed + ref[...]
    parts = LANES // tiles
    sums = jnp.concatenate(
        [packed[:, tiles * q : tiles * (q + 1)] for q in range(parts)], axis=0
    )
    quantity = [sums[sections * q : sections * (q + 1)] for q in range(AHEAD + 2)]
    mean = quantity[0] / samples
    variance = quantity[1] / samples - mean * mean
    place = lax.broadcasted_iota(jnp.int32, (sections, tiles), 0)
    numerator = jnp.zeros((sections, tiles), jnp.float32)
    denominator = jnp.zeros((sections, tiles), jnp.float32)
    knots = knots_ref.shape[0]
    for k in range(1, AHEAD + 1):
        covariance = quantity[k + 1] / samples - mean * shift_up(mean, k)
        correlation = covariance / jnp.sqrt(variance * shift_up(variance, k) + EPSILON)
        distance = jnp.zeros((sections, tiles), jnp.float32)
        for j in range(knots):
            grid = -1.0 + j * (2.0 / (knots - 1))
            hat = jnp.maximum(0.0, 1.0 - jnp.abs(correlation - grid) * ((knots - 1) / 2.0))
            distance = distance + hat * (knots_ref[j].astype(jnp.float32) / 1000.0)
        usable = (place + k < sections).astype(jnp.float32)
        numerator = numerator + usable * (k * distance)
        denominator = denominator + usable * float(k * k)
    thickness = numerator / jnp.maximum(denominator, 1.0)
    depths = [jnp.zeros((1, tiles), jnp.float32)]
    for s in range(sections - 1):
        depths.append(depths[-1] + thickness[s : s + 1])
    row = tile_row_ref[0]
    offset = offset_ref[pl.ds(row, 1), :]
    step = step_ref[pl.ds(row, 1), :]
    index = lax.broadcasted_iota(jnp.int32, (outputs, tiles), 0)
    fraction = (offset + index * step).astype(jnp.float32) / (64.0 * outputs)
    target = depths[-1] * fraction
    bracket = jnp.zeros((outputs, tiles), jnp.int32)
    for s in range(1, sections):
        bracket = bracket + (depths[s] <= target).astype(jnp.int32)
    bracket = jnp.minimum(bracket, sections - 2)
    lower = jnp.zeros((outputs, tiles), jnp.float32)
    upper = jnp.zeros((outputs, tiles), jnp.float32)
    for s in range(sections - 1):
        here = bracket == s
        lower = jnp.where(here, depths[s], lower)
        upper = jnp.where(here, depths[s + 1], upper)
    lifted = bracket.astype(jnp.float32) + (target - lower) / (upper - lower)
    for s in range(sections):
        weights_ref[outputs * s : outputs * (s + 1), :] = jnp.maximum(
            0.0, 1.0 - jnp.abs(lifted - float(s))
        ).astype(jnp.bfloat16)
    to_pixels = one_hot((tiles, cols), lambda r: r, lambda c: c // TILE)
    spread_ref[...] = jnp.dot(
        weights_ref[...], to_pixels, preferred_element_type=jnp.float32
    )

    @pl.loop(0, cols // LANES)
    def _(g):
        lanes = pl.ds(pl.multiple_of(g * LANES, LANES), LANES)
        pixels = [x_ref[s, :, lanes].astype(jnp.float32) for s in range(sections)]
        for j in range(outputs):
            total = jnp.zeros((rows, LANES), jnp.float32)
            for s in range(sections):
                total = total + spread_ref[pl.ds(outputs * s + j, 1), lanes] * pixels[s]
            out_ref[j, :, lanes] = total.astype(jnp.bfloat16)


def per_device(sections, calibration_knots, target_offset, target_step):
    section_total = lax.axis_size("sec")
    position = lax.axis_index("sec")
    row_total, cols = sections.shape[1:]
    rows_local = row_total // section_total
    sharers = TILE // rows_local
    tiles = cols // TILE
    if rows_local % 16 or section_total % 8 or LANES % tiles or cols % (2 * LANES):
        return plain_per_device(
            sections, calibration_knots, target_offset, target_step
        )
    blocks = sections.reshape(section_total, rows_local, cols)
    pencils = lax.all_to_all(blocks, "sec", split_axis=0, concat_axis=0, tiled=True)
    height = (AHEAD + 2) * section_total * tiles // LANES
    vmem = pl.BlockSpec(memory_space=pltpu.VMEM)
    smem = pl.BlockSpec(memory_space=pltpu.SMEM)
    pixels = section_total * rows_local * cols
    partial_sums = pl.pallas_call(
        sums_kernel,
        out_shape=jax.ShapeDtypeStruct((height, LANES), jnp.float32),
        in_specs=[vmem],
        out_specs=vmem,
        scratch_shapes=[
            pltpu.VMEM(
                (cols // 2 // LANES, section_total * rows_local, LANES), jnp.float32
            ),
            pltpu.VMEM(((AHEAD + 2) * section_total, cols // 2), jnp.float32),
        ],
        compiler_params=pltpu.CompilerParams(vmem_limit_bytes=32 * 2**20),
        cost_estimate=pl.CostEstimate(
            flops=pixels * 8, bytes_accessed=pixels * 2, transcendentals=0
        ),
    )(pencils)
    all_sums = [partial_sums]
    for other in range(1, sharers):
        all_sums.append(
            lax.ppermute(
                partial_sums, "sec", [(i, i ^ other) for i in range(section_total)]
            )
        )
    tile_row = (position * rows_local // TILE).astype(jnp.int32).reshape(1)
    return pl.pallas_call(
        resample_kernel,
        out_shape=jax.ShapeDtypeStruct(pencils.shape, jnp.bfloat16),
        in_specs=[smem, smem, vmem, vmem] + [vmem] * sharers + [vmem],
        out_specs=vmem,
        scratch_shapes=[
            pltpu.VMEM((section_total * section_total, tiles), jnp.bfloat16),
            pltpu.VMEM((section_total * section_total, cols), jnp.float32),
        ],
        compiler_params=pltpu.CompilerParams(vmem_limit_bytes=32 * 2**20),
        cost_estimate=pl.CostEstimate(
            flops=pixels * 2 * section_total, bytes_accessed=pixels * 4, transcendentals=0
        ),
    )(tile_row, calibration_knots, target_offset, target_step, *all_sums, pencils)


def solution(mesh):
    return jax.shard_map(
        per_device,
        mesh=mesh,
        in_specs=(P("sec", None, "tile"), P(), P(None, "tile"), P(None, "tile")),
        out_specs=P(None, "sec", "tile"),
        check_vma=False,
    )
```

```python
import functools

import jax
import jax.numpy as jnp
from jax import lax
from jax.experimental import pallas as pl
from jax.experimental.pallas import tpu as pltpu
from jax.sharding import PartitionSpec as P

TILE = 64
AHEAD = 4
LANES = 128
EPSILON = 1e-06


def from_behind(value, axis, steps):
    count = lax.axis_size(axis)
    first, last = (max(0, -steps), min(count, count - steps))
    return lax.ppermute(value, axis, [(source, source + steps) for source in range(first, last)])


def shrink(pixels):
    leading = pixels.shape[:-2]
    row_total = pixels.shape[-2]
    col_total = pixels.shape[-1]
    blocks = pixels.astype(jnp.float32).reshape(leading + (row_total // 2, 2, col_total // 2, 2))
    return jnp.mean(blocks, axis=(-3, -1)).astype(jnp.bfloat16)


def moments(current, following, row_group, half_tile):
    leading = current.shape[:-2]
    tiled_shape = leading + (
        current.shape[-2] // row_group,
        row_group,
        current.shape[-1] // half_tile,
        half_tile,
    )
    first_tile = current.astype(jnp.float32).reshape(tiled_shape)
    second_tile = following.astype(jnp.float32).reshape(tiled_shape)

    def tile_total(values):
        return jnp.sum(values, axis=(-3, -1))

    return (
        tile_total(first_tile),
        tile_total(second_tile),
        tile_total(first_tile * first_tile),
        tile_total(second_tile * second_tile),
        tile_total(first_tile * second_tile),
    )


def correlate(moment_sums, samples):
    sum_first, sum_second, sum_ff, sum_ss, sum_fs = moment_sums
    mean_first = sum_first / samples
    mean_second = sum_second / samples
    covariance = sum_fs / samples - mean_first * mean_second
    var_first = sum_ff / samples - mean_first * mean_first
    var_second = sum_ss / samples - mean_second * mean_second
    return covariance / jnp.sqrt(var_first * var_second + EPSILON)


def calibrate(correlation, knot_values):
    knot_total = knot_values.shape[0]
    knot_grid = -1.0 + jnp.arange(knot_total, dtype=jnp.float32) * (2.0 / (knot_total - 1))
    hat_weights = jnp.maximum(
        0.0, 1.0 - jnp.abs(correlation[..., None] - knot_grid) * ((knot_total - 1) / 2.0)
    )
    return jnp.sum(hat_weights * (knot_values.astype(jnp.float32) / 1000.0), axis=-1)


def exclusive_last(values):
    running = jnp.cumsum(values, axis=-1)
    return jnp.concatenate(
        [jnp.zeros(values.shape[:-1] + (1,), jnp.float32), running[..., :-1]], axis=-1
    )


def resample_weights(depths, offsets, strides, outputs):
    section_total = depths.shape[-1]
    grid_index = jnp.arange(outputs, dtype=jnp.int32)
    fraction = (offsets[..., None] + grid_index * strides[..., None]).astype(jnp.float32) / (
        64.0 * outputs
    )
    target = depths[..., -1:] * fraction
    bracket = jnp.sum((depths[..., None, 1:] <= target[..., None]).astype(jnp.int32), axis=-1)
    bracket = jnp.minimum(bracket, section_total - 2)
    section_places = jnp.arange(section_total, dtype=jnp.int32)
    lower_depth = jnp.sum(
        jnp.where(section_places == bracket[..., None], depths[..., None, :], 0.0), axis=-1
    )
    upper_depth = jnp.sum(
        jnp.where(section_places == bracket[..., None] + 1, depths[..., None, :], 0.0), axis=-1
    )
    lifted = bracket.astype(jnp.float32) + (target - lower_depth) / (upper_depth - lower_depth)
    spread = jnp.abs(lifted[..., None] - section_places.astype(jnp.float32))
    return jnp.maximum(0.0, 1.0 - spread).astype(jnp.bfloat16)


def plain_per_device(sections, calibration_knots, target_offset, target_step):
    section_total = lax.axis_size("sec")
    position = lax.axis_index("sec")
    half_tile = TILE // 2
    samples = float(half_tile * half_tile)
    row_total = sections.shape[1]
    rows_local = row_total // section_total
    tile_rows = row_total // TILE
    tiles_wide = sections.shape[2] // TILE
    tile_row = position * rows_local // TILE
    pencils = lax.all_to_all(sections, "sec", split_axis=1, concat_axis=0, tiled=True)
    reduced = shrink(sections[0])
    numerator = jnp.zeros((tile_rows, tiles_wide), jnp.float32)
    denominator = jnp.zeros((), jnp.float32)
    for spacing in range(1, AHEAD + 1):
        forward = from_behind(reduced, "sec", -spacing)
        correlation = correlate(moments(reduced, forward, half_tile, half_tile), samples)
        usable = (position + spacing < section_total).astype(jnp.float32)
        numerator = numerator + usable * (spacing * calibrate(correlation, calibration_knots))
        denominator = denominator + usable * float(spacing * spacing)
    thickness = numerator / jnp.maximum(denominator, 1.0)
    spread_rows = jnp.repeat(thickness, TILE, axis=0)[None]
    carried_maps = lax.all_to_all(spread_rows, "sec", split_axis=1, concat_axis=0, tiled=True)
    column_maps = jnp.transpose(carried_maps[:, 0, :])
    depths = exclusive_last(column_maps)
    offsets_row = lax.dynamic_index_in_dim(target_offset, tile_row, 0, keepdims=False)
    strides_row = lax.dynamic_index_in_dim(target_step, tile_row, 0, keepdims=False)
    weights = resample_weights(depths, offsets_row, strides_row, section_total)
    pencil_tiles = pencils.reshape(section_total, rows_local, tiles_wide, TILE)
    resampled = jnp.einsum(
        "tjs,srtc->jrtc", weights, pencil_tiles, preferred_element_type=jnp.float32
    )
    return resampled.reshape(section_total, rows_local, sections.shape[2]).astype(jnp.bfloat16)


def one_hot(shape, row_of, col_of):
    rows = lax.broadcasted_iota(jnp.int32, shape, 0)
    cols = lax.broadcasted_iota(jnp.int32, shape, 1)
    return (row_of(rows) == col_of(cols)).astype(jnp.float32).astype(jnp.bfloat16)


def shift_up(values, steps):
    if steps == 0:
        return values
    return jnp.concatenate([values[steps:], jnp.zeros_like(values[:steps])], axis=0)


def split_dot(values, ones):
    high = values.astype(jnp.bfloat16)
    rest = values - high.astype(jnp.float32)
    middle = rest.astype(jnp.bfloat16)
    low = (rest - middle.astype(jnp.float32)).astype(jnp.bfloat16)
    dot = functools.partial(jnp.dot, preferred_element_type=jnp.float32)
    return dot(high, ones) + (dot(middle, ones) + dot(low, ones))


def tables_kernel(
    tile_row_ref,
    knots_ref,
    offset_ref,
    step_ref,
    pairing_ref,
    of_tile_ref,
    to_pixels_ref,
    fraction_ref,
    curve_ref,
):
    pairing_ref[...] = one_hot(pairing_ref.shape, lambda r: r // 2, lambda c: c)
    of_tile_ref[...] = one_hot(
        of_tile_ref.shape, lambda r: r // (TILE // 2), lambda c: c
    )
    to_pixels_ref[...] = one_hot(to_pixels_ref.shape, lambda r: r, lambda c: c // TILE)
    outputs = fraction_ref.shape[0]
    row = tile_row_ref[0]
    offset = offset_ref[pl.ds(row, 1), :]
    step = step_ref[pl.ds(row, 1), :]
    index = lax.broadcasted_iota(jnp.int32, fraction_ref.shape, 0)
    fraction_ref[...] = (offset + index * step).astype(jnp.float32) / (64.0 * outputs)
    for j in range(curve_ref.shape[0]):
        curve_ref[pl.ds(j, 1), :] = jnp.full(
            (1, curve_ref.shape[1]), knots_ref[j].astype(jnp.float32) / 1000.0
        )


def sums_kernel(x_ref, pairing_ref, of_tile_ref, sums_ref, pairs_ref, totals_ref):
    sections, rows, cols = x_ref.shape
    half = cols // 2
    tiles = cols // TILE
    pairing = pairing_ref[...]
    for g in range(half // LANES):
        wide = x_ref[:, :, 2 * LANES * g : 2 * LANES * (g + 1)]
        pairs_ref[g] = jnp.dot(
            wide.reshape(sections * rows, 2 * LANES),
            pairing,
            preferred_element_type=jnp.float32,
        )
    for g in range(half // LANES):
        lanes = pl.ds(LANES * g, LANES)
        totals = [jnp.zeros((sections, LANES), jnp.float32)] * (AHEAD + 2)
        for r in range(rows // 2):
            upper = pairs_ref[g, pl.ds(2 * r, sections, stride=rows), :]
            lower = pairs_ref[g, pl.ds(2 * r + 1, sections, stride=rows), :]
            reduced = ((upper + lower) * 0.25).astype(jnp.bfloat16).astype(jnp.float32)
            totals[0] = totals[0] + reduced
            for k in range(AHEAD + 1):
                totals[k + 1] = totals[k + 1] + reduced * shift_up(reduced, k)
        for q in range(AHEAD + 2):
            totals_ref[sections * q : sections * (q + 1), lanes] = totals[q]
    sums = split_dot(totals_ref[...], of_tile_ref[...])
    wide = LANES // tiles
    height = sums.shape[0] // wide
    for q in range(wide):
        sums_ref[:, tiles * q : tiles * (q + 1)] = sums[height * q : height * (q + 1)]


def resample_kernel(fraction_ref, curve_ref, to_pixels_ref, *refs):
    *sums_refs, x_ref, out_ref, bracket_ref, place_ref, spread_ref, made_ref = refs[:-2]
    place_sem, out_sems = refs[-2:]
    sections, rows, cols = x_ref.shape
    outputs = out_ref.shape[0]
    tiles = cols // TILE
    samples = float((TILE // 2) ** 2)
    packed = sums_refs[0][...]
    for ref in sums_refs[1:]:
        packed = packed + ref[...]
    parts = LANES // tiles
    sums = jnp.concatenate(
        [packed[:, tiles * q : tiles * (q + 1)] for q in range(parts)], axis=0
    )
    quantity = [sums[sections * q : sections * (q + 1)] for q in range(AHEAD + 2)]
    mean = quantity[0] / samples
    variance = quantity[1] / samples - mean * mean
    place = lax.broadcasted_iota(jnp.int32, (sections, tiles), 0)
    numerator = jnp.zeros((sections, tiles), jnp.float32)
    denominator = jnp.zeros((sections, tiles), jnp.float32)
    knots = curve_ref.shape[0]
    for k in range(1, AHEAD + 1):
        covariance = quantity[k + 1] / samples - mean * shift_up(mean, k)
        correlation = covariance / jnp.sqrt(variance * shift_up(variance, k) + EPSILON)
        distance = jnp.zeros((sections, tiles), jnp.float32)
        for j in range(knots):
            grid = -1.0 + j * (2.0 / (knots - 1))
            hat = jnp.maximum(0.0, 1.0 - jnp.abs(correlation - grid) * ((knots - 1) / 2.0))
            distance = distance + hat * curve_ref[j : j + 1, :]
        usable = (place + k < sections).astype(jnp.float32)
        numerator = numerator + usable * (k * distance)
        denominator = denominator + usable * float(k * k)
    thickness = numerator / jnp.maximum(denominator, 1.0)
    depths = [jnp.zeros((1, tiles), jnp.float32)]
    for s in range(sections - 1):
        depths.append(depths[-1] + thickness[s : s + 1])
    target = depths[-1] * fraction_ref[...]
    bracket = jnp.zeros((outputs, tiles), jnp.int32)
    for s in range(1, sections):
        bracket = bracket + (depths[s] <= target).astype(jnp.int32)
    bracket = jnp.minimum(bracket, sections - 2)
    lower = jnp.zeros((outputs, tiles), jnp.float32)
    upper = jnp.zeros((outputs, tiles), jnp.float32)
    for s in range(sections - 1):
        here = bracket == s
        lower = jnp.where(here, depths[s], lower)
        upper = jnp.where(here, depths[s + 1], upper)
    lifted = bracket.astype(jnp.float32) + (target - lower) / (upper - lower)
    bracket_ref[:, :tiles] = bracket
    to_smem = pltpu.make_async_copy(bracket_ref, place_ref, place_sem)
    to_smem.start()
    beyond = lifted - bracket.astype(jnp.float32)
    pair = jnp.concatenate(
        [1.0 - jnp.abs(beyond), jnp.maximum(0.0, 1.0 - jnp.abs(beyond - 1.0))], axis=0
    )
    spread_ref[...] = jnp.dot(
        jnp.maximum(0.0, pair).astype(jnp.bfloat16),
        to_pixels_ref[...],
        preferred_element_type=jnp.float32,
    )
    to_smem.wait()
    first = lax.broadcasted_iota(jnp.int32, (rows, LANES), 1) < TILE

    def to_hbm(j):
        return pltpu.make_async_copy(made_ref.at[j], out_ref.at[j], out_sems.at[j])

    for j in range(outputs):
        for g in range(cols // LANES):
            lanes = pl.ds(g * LANES, LANES)
            left = place_ref[j, 2 * g]
            right = place_ref[j, 2 * g + 1]
            near = jnp.where(first, x_ref[left, :, lanes], x_ref[right, :, lanes])
            far = jnp.where(
                first, x_ref[left + 1, :, lanes], x_ref[right + 1, :, lanes]
            )
            made_ref[j, :, lanes] = (
                spread_ref[pl.ds(j, 1), lanes] * near.astype(jnp.float32)
                + spread_ref[pl.ds(outputs + j, 1), lanes] * far.astype(jnp.float32)
            ).astype(jnp.bfloat16)
        to_hbm(j).start()

    for j in range(outputs):
        to_hbm(j).wait()


def per_device(sections, calibration_knots, target_offset, target_step):
    section_total = lax.axis_size("sec")
    position = lax.axis_index("sec")
    row_total, cols = sections.shape[1:]
    rows_local = row_total // section_total
    sharers = TILE // rows_local
    tiles = cols // TILE
    if rows_local % 16 or section_total % 8 or LANES % tiles or cols % (2 * LANES):
        return plain_per_device(
            sections, calibration_knots, target_offset, target_step
        )
    blocks = sections.reshape(section_total, rows_local, cols)
    pencils = lax.all_to_all(blocks, "sec", split_axis=0, concat_axis=0, tiled=True)
    height = (AHEAD + 2) * section_total * tiles // LANES
    vmem = pl.BlockSpec(memory_space=pltpu.VMEM)
    smem = pl.BlockSpec(memory_space=pltpu.SMEM)
    pixels = section_total * rows_local * cols
    tile_row = (position * rows_local // TILE).astype(jnp.int32).reshape(1)
    pairing, of_tile, to_pixels, fraction, curve = pl.pallas_call(
        tables_kernel,
        out_shape=[
            jax.ShapeDtypeStruct((2 * LANES, LANES), jnp.bfloat16),
            jax.ShapeDtypeStruct((cols // 2, tiles), jnp.bfloat16),
            jax.ShapeDtypeStruct((tiles, cols), jnp.bfloat16),
            jax.ShapeDtypeStruct((section_total, tiles), jnp.float32),
            jax.ShapeDtypeStruct((calibration_knots.shape[0], tiles), jnp.float32),
        ],
        in_specs=[smem, smem, vmem, vmem],
        out_specs=[vmem] * 5,
        compiler_params=pltpu.CompilerParams(vmem_limit_bytes=4 * 2**20),
        cost_estimate=pl.CostEstimate(
            flops=2**20, bytes_accessed=2**20, transcendentals=0
        ),
    )(tile_row, calibration_knots, target_offset, target_step)
    partial_sums = pl.pallas_call(
        sums_kernel,
        out_shape=jax.ShapeDtypeStruct((height, LANES), jnp.float32),
        in_specs=[vmem] * 3,
        out_specs=vmem,
        scratch_shapes=[
            pltpu.VMEM(
                (cols // 2 // LANES, section_total * rows_local, LANES), jnp.float32
            ),
            pltpu.VMEM(((AHEAD + 2) * section_total, cols // 2), jnp.float32),
        ],
        compiler_params=pltpu.CompilerParams(vmem_limit_bytes=16 * 2**20),
        cost_estimate=pl.CostEstimate(
            flops=pixels * 8, bytes_accessed=pixels * 2, transcendentals=0
        ),
    )(pencils, pairing, of_tile)
    all_sums = [partial_sums]
    for other in range(1, sharers):
        all_sums.append(
            lax.ppermute(
                partial_sums, "sec", [(i, i ^ other) for i in range(section_total)]
            )
        )
    return pl.pallas_call(
        resample_kernel,
        out_shape=jax.ShapeDtypeStruct(pencils.shape, jnp.bfloat16),
        in_specs=[vmem] * (sharers + 4),
        out_specs=pl.BlockSpec(memory_space=pl.ANY),
        scratch_shapes=[
            pltpu.VMEM((section_total, LANES), jnp.int32),
            pltpu.SMEM((section_total, LANES), jnp.int32),
            pltpu.VMEM((2 * section_total, cols), jnp.float32),
            pltpu.VMEM(pencils.shape, jnp.bfloat16),
            pltpu.SemaphoreType.DMA,
            pltpu.SemaphoreType.DMA((section_total,)),
        ],
        compiler_params=pltpu.CompilerParams(vmem_limit_bytes=16 * 2**20),
        cost_estimate=pl.CostEstimate(
            flops=pixels * 2 * section_total, bytes_accessed=pixels * 4, transcendentals=0
        ),
    )(fraction, curve, to_pixels, *all_sums, pencils)


def solution(mesh):
    return jax.shard_map(
        per_device,
        mesh=mesh,
        in_specs=(P("sec", None, "tile"), P(), P(None, "tile"), P(None, "tile")),
        out_specs=P(None, "sec", "tile"),
        check_vma=False,
    )
```

```python
import functools

import jax
import jax.numpy as jnp
from jax import lax
from jax.experimental import pallas as pl
from jax.experimental.pallas import tpu as pltpu
from jax.sharding import PartitionSpec as P

TILE = 64
AHEAD = 4
LANES = 128
EPSILON = 1e-06


def from_behind(value, axis, steps):
    count = lax.axis_size(axis)
    first, last = (max(0, -steps), min(count, count - steps))
    return lax.ppermute(value, axis, [(source, source + steps) for source in range(first, last)])


def shrink(pixels):
    leading = pixels.shape[:-2]
    row_total = pixels.shape[-2]
    col_total = pixels.shape[-1]
    blocks = pixels.astype(jnp.float32).reshape(leading + (row_total // 2, 2, col_total // 2, 2))
    return jnp.mean(blocks, axis=(-3, -1)).astype(jnp.bfloat16)


def moments(current, following, row_group, half_tile):
    leading = current.shape[:-2]
    tiled_shape = leading + (
        current.shape[-2] // row_group,
        row_group,
        current.shape[-1] // half_tile,
        half_tile,
    )
    first_tile = current.astype(jnp.float32).reshape(tiled_shape)
    second_tile = following.astype(jnp.float32).reshape(tiled_shape)

    def tile_total(values):
        return jnp.sum(values, axis=(-3, -1))

    return (
        tile_total(first_tile),
        tile_total(second_tile),
        tile_total(first_tile * first_tile),
        tile_total(second_tile * second_tile),
        tile_total(first_tile * second_tile),
    )


def correlate(moment_sums, samples):
    sum_first, sum_second, sum_ff, sum_ss, sum_fs = moment_sums
    mean_first = sum_first / samples
    mean_second = sum_second / samples
    covariance = sum_fs / samples - mean_first * mean_second
    var_first = sum_ff / samples - mean_first * mean_first
    var_second = sum_ss / samples - mean_second * mean_second
    return covariance / jnp.sqrt(var_first * var_second + EPSILON)


def calibrate(correlation, knot_values):
    knot_total = knot_values.shape[0]
    knot_grid = -1.0 + jnp.arange(knot_total, dtype=jnp.float32) * (2.0 / (knot_total - 1))
    hat_weights = jnp.maximum(
        0.0, 1.0 - jnp.abs(correlation[..., None] - knot_grid) * ((knot_total - 1) / 2.0)
    )
    return jnp.sum(hat_weights * (knot_values.astype(jnp.float32) / 1000.0), axis=-1)


def exclusive_last(values):
    running = jnp.cumsum(values, axis=-1)
    return jnp.concatenate(
        [jnp.zeros(values.shape[:-1] + (1,), jnp.float32), running[..., :-1]], axis=-1
    )


def resample_weights(depths, offsets, strides, outputs):
    section_total = depths.shape[-1]
    grid_index = jnp.arange(outputs, dtype=jnp.int32)
    fraction = (offsets[..., None] + grid_index * strides[..., None]).astype(jnp.float32) / (
        64.0 * outputs
    )
    target = depths[..., -1:] * fraction
    bracket = jnp.sum((depths[..., None, 1:] <= target[..., None]).astype(jnp.int32), axis=-1)
    bracket = jnp.minimum(bracket, section_total - 2)
    section_places = jnp.arange(section_total, dtype=jnp.int32)
    lower_depth = jnp.sum(
        jnp.where(section_places == bracket[..., None], depths[..., None, :], 0.0), axis=-1
    )
    upper_depth = jnp.sum(
        jnp.where(section_places == bracket[..., None] + 1, depths[..., None, :], 0.0), axis=-1
    )
    lifted = bracket.astype(jnp.float32) + (target - lower_depth) / (upper_depth - lower_depth)
    spread = jnp.abs(lifted[..., None] - section_places.astype(jnp.float32))
    return jnp.maximum(0.0, 1.0 - spread).astype(jnp.bfloat16)


def plain_per_device(sections, calibration_knots, target_offset, target_step):
    section_total = lax.axis_size("sec")
    position = lax.axis_index("sec")
    half_tile = TILE // 2
    samples = float(half_tile * half_tile)
    row_total = sections.shape[1]
    rows_local = row_total // section_total
    tile_rows = row_total // TILE
    tiles_wide = sections.shape[2] // TILE
    tile_row = position * rows_local // TILE
    pencils = lax.all_to_all(sections, "sec", split_axis=1, concat_axis=0, tiled=True)
    reduced = shrink(sections[0])
    numerator = jnp.zeros((tile_rows, tiles_wide), jnp.float32)
    denominator = jnp.zeros((), jnp.float32)
    for spacing in range(1, AHEAD + 1):
        forward = from_behind(reduced, "sec", -spacing)
        correlation = correlate(moments(reduced, forward, half_tile, half_tile), samples)
        usable = (position + spacing < section_total).astype(jnp.float32)
        numerator = numerator + usable * (spacing * calibrate(correlation, calibration_knots))
        denominator = denominator + usable * float(spacing * spacing)
    thickness = numerator / jnp.maximum(denominator, 1.0)
    spread_rows = jnp.repeat(thickness, TILE, axis=0)[None]
    carried_maps = lax.all_to_all(spread_rows, "sec", split_axis=1, concat_axis=0, tiled=True)
    column_maps = jnp.transpose(carried_maps[:, 0, :])
    depths = exclusive_last(column_maps)
    offsets_row = lax.dynamic_index_in_dim(target_offset, tile_row, 0, keepdims=False)
    strides_row = lax.dynamic_index_in_dim(target_step, tile_row, 0, keepdims=False)
    weights = resample_weights(depths, offsets_row, strides_row, section_total)
    pencil_tiles = pencils.reshape(section_total, rows_local, tiles_wide, TILE)
    resampled = jnp.einsum(
        "tjs,srtc->jrtc", weights, pencil_tiles, preferred_element_type=jnp.float32
    )
    return resampled.reshape(section_total, rows_local, sections.shape[2]).astype(jnp.bfloat16)


def one_hot(shape, row_of, col_of):
    rows = lax.broadcasted_iota(jnp.int32, shape, 0)
    cols = lax.broadcasted_iota(jnp.int32, shape, 1)
    return (row_of(rows) == col_of(cols)).astype(jnp.float32).astype(jnp.bfloat16)


def shift_up(values, steps):
    if steps == 0:
        return values
    return jnp.concatenate([values[steps:], jnp.zeros_like(values[:steps])], axis=0)


def tile_of_lane(lanes):
    group = (lanes // 16) % 2 + 2 * ((lanes // 8) % 2) + 4 * ((lanes // 4) % 2)
    return lanes // 32 + 4 * group


def lane_of_tile(tile):
    group = tile // 4
    return 32 * (tile % 4) + 16 * (group % 2) + 8 * (group // 2 % 2) + 4 * (group // 4)


def tables_kernel(
    tile_row_ref,
    knots_ref,
    offset_ref,
    step_ref,
    pairing_ref,
    to_pixels_ref,
    fraction_ref,
    curve_ref,
):
    pairing_ref[...] = one_hot(pairing_ref.shape, lambda r: r // 2, lambda c: c)
    to_pixels_ref[...] = one_hot(
        to_pixels_ref.shape,
        lambda r: jnp.where(r % 4 == 0, tile_of_lane(r), -1),
        lambda c: c // TILE,
    )
    outputs = fraction_ref.shape[0]
    row = tile_row_ref[0]
    to_lanes = one_hot(
        (offset_ref.shape[1], LANES), lambda r: r, lambda c: tile_of_lane(c)
    )

    def spread(ref):
        values = jnp.broadcast_to(ref[pl.ds(row, 1), :], (16, ref.shape[1]))
        return jnp.dot(
            values.astype(jnp.float32).astype(jnp.bfloat16),
            to_lanes,
            preferred_element_type=jnp.float32,
        )[:1]

    index = lax.broadcasted_iota(jnp.int32, fraction_ref.shape, 0).astype(jnp.float32)
    fraction_ref[...] = (spread(offset_ref) + index * spread(step_ref)) / (
        64.0 * outputs
    )
    for j in range(curve_ref.shape[0]):
        curve_ref[pl.ds(j, 1), :] = jnp.full(
            (1, curve_ref.shape[1]), knots_ref[j].astype(jnp.float32) / 1000.0
        )


def fold(first, second, width, lanes):
    return jnp.where(
        (lanes // width) % 2 == 0,
        first + pltpu.roll(first, LANES - width, 1),
        second + pltpu.roll(second, width, 1),
    )


def sums_kernel(x_ref, pairing_ref, sums_ref, pairs_ref, reduced_ref):
    sections, rows, cols = x_ref.shape
    groups = cols // 2 // LANES
    pairing = pairing_ref[...]
    for g in range(groups):
        wide = x_ref[:, :, 2 * LANES * g : 2 * LANES * (g + 1)]
        pairs = jnp.dot(
            wide.reshape(sections * rows, 2 * LANES),
            pairing,
            preferred_element_type=jnp.float32,
        )
        for s in range(sections):
            pairs_ref[g, pl.ds(17 * s, rows), :] = pairs[rows * s : rows * (s + 1)]
    lanes = lax.broadcasted_iota(jnp.int32, (sections, LANES), 1)
    waiting = {}
    for g in range(groups):
        total = [jnp.zeros((sections, LANES), jnp.float32)] * (AHEAD + 2)
        for r in range(rows // 2):
            upper = pairs_ref[g, pl.ds(2 * r, sections, stride=17), :]
            lower = pairs_ref[g, pl.ds(2 * r + 1, sections, stride=17), :]
            reduced = ((upper + lower) * 0.25).astype(jnp.bfloat16).astype(jnp.float32)
            reduced_ref[g, r, :sections] = reduced
            reduced_ref[g, r, sections:] = jnp.zeros((8, LANES), jnp.float32)
            total[0] = total[0] + reduced
            total[1] = total[1] + reduced * reduced
            for k in range(1, AHEAD + 1):
                total[k + 1] = total[k + 1] + reduced * reduced_ref[g, r, k : k + sections]
        width = 16
        while (g * width // 16) % 2 == 1 and width >= 4:
            total = [fold(a, b, width, lanes) for a, b in zip(waiting.pop(width), total)]
            width //= 2
        waiting[width] = total
    total = waiting.pop(2)
    for v in range((AHEAD + 2) // 2):
        pair = fold(total[2 * v], total[2 * v + 1], 2, lanes)
        sums_ref[8 * v : 8 * v + 8] = fold(pair[:8], pair[8:], 1, lanes[:8])


def resample_kernel(fraction_ref, curve_ref, to_pixels_ref, *refs):
    *sums_refs, x_ref, out_ref, spread_ref, made_ref, out_sems = refs
    sections, rows, cols = x_ref.shape
    outputs = out_ref.shape[0]
    tiles = LANES
    samples = float((TILE // 2) ** 2)
    packed = sums_refs[0][...]
    for ref in sums_refs[1:]:
        packed = packed + ref[...]

    def unpack(q, half):
        part = packed[8 * (q // 2) : 8 * (q // 2) + 8]
        b = 2 * (q % 2) + half
        return pltpu.roll(part, LANES - b, 1) if b else part

    quantity = [
        jnp.concatenate([unpack(q, 0), unpack(q, 1)], axis=0) for q in range(AHEAD + 2)
    ]
    mean = quantity[0] / samples
    variance = quantity[1] / samples - mean * mean
    place = lax.broadcasted_iota(jnp.int32, (sections, tiles), 0)
    numerator = jnp.zeros((sections, tiles), jnp.float32)
    denominator = jnp.zeros((sections, tiles), jnp.float32)
    knots = curve_ref.shape[0]
    for k in range(1, AHEAD + 1):
        covariance = quantity[k + 1] / samples - mean * shift_up(mean, k)
        correlation = covariance / jnp.sqrt(variance * shift_up(variance, k) + EPSILON)
        distance = jnp.zeros((sections, tiles), jnp.float32)
        for j in range(knots):
            grid = -1.0 + j * (2.0 / (knots - 1))
            hat = jnp.maximum(0.0, 1.0 - jnp.abs(correlation - grid) * ((knots - 1) / 2.0))
            distance = distance + hat * curve_ref[j : j + 1, :]
        usable = (place + k < sections).astype(jnp.float32)
        numerator = numerator + usable * (k * distance)
        denominator = denominator + usable * float(k * k)
    thickness = numerator / jnp.maximum(denominator, 1.0)
    depths = [jnp.zeros((1, tiles), jnp.float32)]
    for s in range(sections - 1):
        depths.append(depths[-1] + thickness[s : s + 1])
    target = depths[-1] * fraction_ref[...]
    bracket = jnp.zeros((outputs, tiles), jnp.int32)
    for s in range(1, sections):
        bracket = bracket + (depths[s] <= target).astype(jnp.int32)
    bracket = jnp.minimum(bracket, sections - 2)
    lower = jnp.zeros((outputs, tiles), jnp.float32)
    upper = jnp.zeros((outputs, tiles), jnp.float32)
    for s in range(sections - 1):
        here = bracket == s
        lower = jnp.where(here, depths[s], lower)
        upper = jnp.where(here, depths[s + 1], upper)
    lifted = bracket.astype(jnp.float32) + (target - lower) / (upper - lower)
    beyond = lifted - bracket.astype(jnp.float32)
    pair = jnp.concatenate(
        [1.0 - jnp.abs(beyond), jnp.maximum(0.0, 1.0 - jnp.abs(beyond - 1.0))], axis=0
    )
    used = lax.broadcasted_iota(jnp.int32, pair.shape, 1) % 4 == 0
    spread_ref[...] = jnp.dot(
        jnp.where(used, jnp.maximum(0.0, pair), 0.0).astype(jnp.bfloat16),
        to_pixels_ref[...],
        preferred_element_type=jnp.float32,
    )
    first = lax.broadcasted_iota(jnp.int32, (rows, LANES), 1) < TILE

    def to_hbm(j):
        return pltpu.make_async_copy(made_ref.at[j], out_ref.at[j], out_sems.at[j])

    for j in range(outputs):
        for g in range(cols // LANES):
            lanes = pl.ds(g * LANES, LANES)
            left = bracket[j, lane_of_tile(2 * g)]
            right = bracket[j, lane_of_tile(2 * g + 1)]
            near = jnp.where(first, x_ref[left, :, lanes], x_ref[right, :, lanes])
            far = jnp.where(
                first, x_ref[left + 1, :, lanes], x_ref[right + 1, :, lanes]
            )
            made_ref[j, :, lanes] = (
                spread_ref[pl.ds(j, 1), lanes] * near.astype(jnp.float32)
                + spread_ref[pl.ds(outputs + j, 1), lanes] * far.astype(jnp.float32)
            ).astype(jnp.bfloat16)
        to_hbm(j).start()

    for j in range(outputs):
        to_hbm(j).wait()


def per_device(sections, calibration_knots, target_offset, target_step):
    section_total = lax.axis_size("sec")
    position = lax.axis_index("sec")
    row_total, cols = sections.shape[1:]
    rows_local = row_total // section_total
    sharers = TILE // rows_local
    tiles = cols // TILE
    if rows_local % 16 or section_total != 16 or tiles * 4 != LANES or sharers > 16:
        return plain_per_device(
            sections, calibration_knots, target_offset, target_step
        )
    blocks = sections.reshape(section_total, rows_local, cols)
    pencils = lax.all_to_all(blocks, "sec", split_axis=0, concat_axis=0, tiled=True)
    height = 8 * (AHEAD + 2) // 2
    vmem = pl.BlockSpec(memory_space=pltpu.VMEM)
    smem = pl.BlockSpec(memory_space=pltpu.SMEM)
    pixels = section_total * rows_local * cols
    tile_row = (position * rows_local // TILE).astype(jnp.int32).reshape(1)
    pairing, to_pixels, fraction, curve = pl.pallas_call(
        tables_kernel,
        out_shape=[
            jax.ShapeDtypeStruct((2 * LANES, LANES), jnp.bfloat16),
            jax.ShapeDtypeStruct((LANES, cols), jnp.bfloat16),
            jax.ShapeDtypeStruct((section_total, LANES), jnp.float32),
            jax.ShapeDtypeStruct((calibration_knots.shape[0], LANES), jnp.float32),
        ],
        in_specs=[smem, smem, vmem, vmem],
        out_specs=[vmem] * 4,
        compiler_params=pltpu.CompilerParams(vmem_limit_bytes=4 * 2**20),
        cost_estimate=pl.CostEstimate(
            flops=2**20, bytes_accessed=2**20, transcendentals=0
        ),
    )(tile_row, calibration_knots, target_offset, target_step)
    partial_sums = pl.pallas_call(
        sums_kernel,
        out_shape=jax.ShapeDtypeStruct((height, LANES), jnp.float32),
        in_specs=[vmem] * 2,
        out_specs=vmem,
        scratch_shapes=[
            pltpu.VMEM(
                (cols // 2 // LANES, section_total * 17, LANES), jnp.float32
            ),
            pltpu.VMEM(
                (cols // 2 // LANES, rows_local // 2, section_total + 8, LANES),
                jnp.float32,
            ),
        ],
        compiler_params=pltpu.CompilerParams(vmem_limit_bytes=16 * 2**20),
        cost_estimate=pl.CostEstimate(
            flops=pixels * 8, bytes_accessed=pixels * 2, transcendentals=0
        ),
    )(pencils, pairing)
    all_sums = [partial_sums]
    for other in range(1, sharers):
        all_sums.append(
            lax.ppermute(
                partial_sums, "sec", [(i, i ^ other) for i in range(section_total)]
            )
        )
    return pl.pallas_call(
        resample_kernel,
        out_shape=jax.ShapeDtypeStruct(pencils.shape, jnp.bfloat16),
        in_specs=[vmem] * (sharers + 4),
        out_specs=pl.BlockSpec(memory_space=pl.ANY),
        scratch_shapes=[
            pltpu.VMEM((2 * section_total, cols), jnp.float32),
            pltpu.VMEM(pencils.shape, jnp.bfloat16),
            pltpu.SemaphoreType.DMA((section_total,)),
        ],
        compiler_params=pltpu.CompilerParams(vmem_limit_bytes=16 * 2**20),
        cost_estimate=pl.CostEstimate(
            flops=pixels * 2 * section_total, bytes_accessed=pixels * 4, transcendentals=0
        ),
    )(fraction, curve, to_pixels, *all_sums, pencils)


def solution(mesh):
    return jax.shard_map(
        per_device,
        mesh=mesh,
        in_specs=(P("sec", None, "tile"), P(), P(None, "tile"), P(None, "tile")),
        out_specs=P(None, "sec", "tile"),
        check_vma=False,
    )
```

```python
import functools

import jax
import jax.numpy as jnp
from jax import lax
from jax.experimental import pallas as pl
from jax.experimental.pallas import tpu as pltpu
from jax.sharding import PartitionSpec as P

TILE = 64
AHEAD = 4
LANES = 128
EPSILON = 1e-06


def from_behind(value, axis, steps):
    count = lax.axis_size(axis)
    first, last = (max(0, -steps), min(count, count - steps))
    return lax.ppermute(value, axis, [(source, source + steps) for source in range(first, last)])


def shrink(pixels):
    leading = pixels.shape[:-2]
    row_total = pixels.shape[-2]
    col_total = pixels.shape[-1]
    blocks = pixels.astype(jnp.float32).reshape(leading + (row_total // 2, 2, col_total // 2, 2))
    return jnp.mean(blocks, axis=(-3, -1)).astype(jnp.bfloat16)


def moments(current, following, row_group, half_tile):
    leading = current.shape[:-2]
    tiled_shape = leading + (
        current.shape[-2] // row_group,
        row_group,
        current.shape[-1] // half_tile,
        half_tile,
    )
    first_tile = current.astype(jnp.float32).reshape(tiled_shape)
    second_tile = following.astype(jnp.float32).reshape(tiled_shape)

    def tile_total(values):
        return jnp.sum(values, axis=(-3, -1))

    return (
        tile_total(first_tile),
        tile_total(second_tile),
        tile_total(first_tile * first_tile),
        tile_total(second_tile * second_tile),
        tile_total(first_tile * second_tile),
    )


def correlate(moment_sums, samples):
    sum_first, sum_second, sum_ff, sum_ss, sum_fs = moment_sums
    mean_first = sum_first / samples
    mean_second = sum_second / samples
    covariance = sum_fs / samples - mean_first * mean_second
    var_first = sum_ff / samples - mean_first * mean_first
    var_second = sum_ss / samples - mean_second * mean_second
    return covariance / jnp.sqrt(var_first * var_second + EPSILON)


def calibrate(correlation, knot_values):
    knot_total = knot_values.shape[0]
    knot_grid = -1.0 + jnp.arange(knot_total, dtype=jnp.float32) * (2.0 / (knot_total - 1))
    hat_weights = jnp.maximum(
        0.0, 1.0 - jnp.abs(correlation[..., None] - knot_grid) * ((knot_total - 1) / 2.0)
    )
    return jnp.sum(hat_weights * (knot_values.astype(jnp.float32) / 1000.0), axis=-1)


def exclusive_last(values):
    running = jnp.cumsum(values, axis=-1)
    return jnp.concatenate(
        [jnp.zeros(values.shape[:-1] + (1,), jnp.float32), running[..., :-1]], axis=-1
    )


def resample_weights(depths, offsets, strides, outputs):
    section_total = depths.shape[-1]
    grid_index = jnp.arange(outputs, dtype=jnp.int32)
    fraction = (offsets[..., None] + grid_index * strides[..., None]).astype(jnp.float32) / (
        64.0 * outputs
    )
    target = depths[..., -1:] * fraction
    bracket = jnp.sum((depths[..., None, 1:] <= target[..., None]).astype(jnp.int32), axis=-1)
    bracket = jnp.minimum(bracket, section_total - 2)
    section_places = jnp.arange(section_total, dtype=jnp.int32)
    lower_depth = jnp.sum(
        jnp.where(section_places == bracket[..., None], depths[..., None, :], 0.0), axis=-1
    )
    upper_depth = jnp.sum(
        jnp.where(section_places == bracket[..., None] + 1, depths[..., None, :], 0.0), axis=-1
    )
    lifted = bracket.astype(jnp.float32) + (target - lower_depth) / (upper_depth - lower_depth)
    spread = jnp.abs(lifted[..., None] - section_places.astype(jnp.float32))
    return jnp.maximum(0.0, 1.0 - spread).astype(jnp.bfloat16)


def plain_per_device(sections, calibration_knots, target_offset, target_step):
    section_total = lax.axis_size("sec")
    position = lax.axis_index("sec")
    half_tile = TILE // 2
    samples = float(half_tile * half_tile)
    row_total = sections.shape[1]
    rows_local = row_total // section_total
    tile_rows = row_total // TILE
    tiles_wide = sections.shape[2] // TILE
    tile_row = position * rows_local // TILE
    pencils = lax.all_to_all(sections, "sec", split_axis=1, concat_axis=0, tiled=True)
    reduced = shrink(sections[0])
    numerator = jnp.zeros((tile_rows, tiles_wide), jnp.float32)
    denominator = jnp.zeros((), jnp.float32)
    for spacing in range(1, AHEAD + 1):
        forward = from_behind(reduced, "sec", -spacing)
        correlation = correlate(moments(reduced, forward, half_tile, half_tile), samples)
        usable = (position + spacing < section_total).astype(jnp.float32)
        numerator = numerator + usable * (spacing * calibrate(correlation, calibration_knots))
        denominator = denominator + usable * float(spacing * spacing)
    thickness = numerator / jnp.maximum(denominator, 1.0)
    spread_rows = jnp.repeat(thickness, TILE, axis=0)[None]
    carried_maps = lax.all_to_all(spread_rows, "sec", split_axis=1, concat_axis=0, tiled=True)
    column_maps = jnp.transpose(carried_maps[:, 0, :])
    depths = exclusive_last(column_maps)
    offsets_row = lax.dynamic_index_in_dim(target_offset, tile_row, 0, keepdims=False)
    strides_row = lax.dynamic_index_in_dim(target_step, tile_row, 0, keepdims=False)
    weights = resample_weights(depths, offsets_row, strides_row, section_total)
    pencil_tiles = pencils.reshape(section_total, rows_local, tiles_wide, TILE)
    resampled = jnp.einsum(
        "tjs,srtc->jrtc", weights, pencil_tiles, preferred_element_type=jnp.float32
    )
    return resampled.reshape(section_total, rows_local, sections.shape[2]).astype(jnp.bfloat16)


def one_hot(shape, row_of, col_of):
    rows = lax.broadcasted_iota(jnp.int32, shape, 0)
    cols = lax.broadcasted_iota(jnp.int32, shape, 1)
    return (row_of(rows) == col_of(cols)).astype(jnp.float32).astype(jnp.bfloat16)


def shift_up(values, steps):
    if steps == 0:
        return values
    return jnp.concatenate([values[steps:], jnp.zeros_like(values[:steps])], axis=0)


def tile_of_lane(lanes):
    group = (lanes // 16) % 2 + 2 * ((lanes // 8) % 2) + 4 * ((lanes // 4) % 2)
    return lanes // 32 + 4 * group


def lane_of_tile(tile):
    group = tile // 4
    return 32 * (tile % 4) + 16 * (group % 2) + 8 * (group // 2 % 2) + 4 * (group // 4)


def tables_kernel(
    tile_row_ref,
    knots_ref,
    offset_ref,
    step_ref,
    pairing_ref,
    to_pixels_ref,
    fraction_ref,
    curve_ref,
):
    pairing_ref[...] = one_hot(pairing_ref.shape, lambda r: r // 2, lambda c: c)
    to_pixels_ref[...] = one_hot(
        to_pixels_ref.shape,
        lambda r: jnp.where(r % 4 == 0, tile_of_lane(r), -1),
        lambda c: c // TILE,
    )
    outputs = fraction_ref.shape[0]
    row = tile_row_ref[0]
    to_lanes = one_hot(
        (offset_ref.shape[1], LANES), lambda r: r, lambda c: tile_of_lane(c)
    )

    def spread(ref):
        values = jnp.broadcast_to(ref[pl.ds(row, 1), :], (16, ref.shape[1]))
        return jnp.dot(
            values.astype(jnp.float32).astype(jnp.bfloat16),
            to_lanes,
            preferred_element_type=jnp.float32,
        )[:1]

    index = lax.broadcasted_iota(jnp.int32, fraction_ref.shape, 0).astype(jnp.float32)
    fraction_ref[...] = (spread(offset_ref) + index * spread(step_ref)) / (
        64.0 * outputs
    )
    for j in range(curve_ref.shape[0]):
        curve_ref[pl.ds(j, 1), :] = jnp.full(
            (1, curve_ref.shape[1]), knots_ref[j].astype(jnp.float32) / 1000.0
        )


def fold(first, second, width, lanes):
    return jnp.where(
        (lanes // width) % 2 == 0,
        first + pltpu.roll(first, LANES - width, 1),
        second + pltpu.roll(second, width, 1),
    )


def sums_kernel(x_ref, pairing_ref, sums_ref, pairs_ref, reduced_ref):
    sections, rows, cols = x_ref.shape
    groups = cols // 2 // LANES
    pairing = pairing_ref[...]
    for g in range(groups):
        wide = x_ref[:, :, 2 * LANES * g : 2 * LANES * (g + 1)]
        pairs = jnp.dot(
            wide.reshape(sections * rows, 2 * LANES),
            pairing,
            preferred_element_type=jnp.float32,
        )
        for s in range(sections):
            pairs_ref[g, pl.ds(17 * s, rows), :] = pairs[rows * s : rows * (s + 1)]
    lanes = lax.broadcasted_iota(jnp.int32, (sections, LANES), 1)
    waiting = {}
    for g in range(groups):
        total = [jnp.zeros((sections, LANES), jnp.float32)] * (AHEAD + 2)
        for r in range(rows // 2):
            upper = pairs_ref[g, pl.ds(2 * r, sections, stride=17), :]
            lower = pairs_ref[g, pl.ds(2 * r + 1, sections, stride=17), :]
            reduced = ((upper + lower) * 0.25).astype(jnp.bfloat16).astype(jnp.float32)
            reduced_ref[g, r, :sections] = reduced
            reduced_ref[g, r, sections:] = jnp.zeros((8, LANES), jnp.float32)
            total[0] = total[0] + reduced
            total[1] = total[1] + reduced * reduced
            for k in range(1, AHEAD + 1):
                total[k + 1] = total[k + 1] + reduced * reduced_ref[g, r, k : k + sections]
        width = 16
        while (g * width // 16) % 2 == 1 and width >= 4:
            total = [fold(a, b, width, lanes) for a, b in zip(waiting.pop(width), total)]
            width //= 2
        waiting[width] = total
    total = waiting.pop(2)
    for v in range((AHEAD + 2) // 2):
        pair = fold(total[2 * v], total[2 * v + 1], 2, lanes)
        sums_ref[8 * v : 8 * v + 8] = fold(pair[:8], pair[8:], 1, lanes[:8])


def resample_kernel(fraction_ref, curve_ref, to_pixels_ref, *refs):
    *sums_refs, x_ref, out_ref, spread_ref, made_ref, out_sems = refs
    sections, rows, cols = x_ref.shape
    outputs = out_ref.shape[0]
    tiles = LANES
    samples = float((TILE // 2) ** 2)
    packed = sums_refs[0][...]
    for ref in sums_refs[1:]:
        packed = packed + ref[...]

    def unpack(q, half):
        part = packed[8 * (q // 2) : 8 * (q // 2) + 8]
        b = 2 * (q % 2) + half
        return pltpu.roll(part, LANES - b, 1) if b else part

    quantity = [
        jnp.concatenate([unpack(q, 0), unpack(q, 1)], axis=0) for q in range(AHEAD + 2)
    ]
    mean = quantity[0] / samples
    variance = quantity[1] / samples - mean * mean
    place = lax.broadcasted_iota(jnp.int32, (sections, tiles), 0)
    numerator = jnp.zeros((sections, tiles), jnp.float32)
    denominator = jnp.zeros((sections, tiles), jnp.float32)
    knots = curve_ref.shape[0]
    for k in range(1, AHEAD + 1):
        covariance = quantity[k + 1] / samples - mean * shift_up(mean, k)
        correlation = covariance / jnp.sqrt(variance * shift_up(variance, k) + EPSILON)
        distance = jnp.zeros((sections, tiles), jnp.float32)
        scaled = correlation * ((knots - 1) / 2.0)
        for j in range(knots):
            hat = jnp.maximum(0.0, 1.0 - jnp.abs(scaled - (j - (knots - 1) / 2.0)))
            distance = distance + hat * curve_ref[j : j + 1, :]
        usable = (place + k < sections).astype(jnp.float32)
        numerator = numerator + usable * (k * distance)
        denominator = denominator + usable * float(k * k)
    thickness = numerator / jnp.maximum(denominator, 1.0)
    depths = [jnp.zeros((1, tiles), jnp.float32)]
    for s in range(sections - 1):
        depths.append(depths[-1] + thickness[s : s + 1])
    target = depths[-1] * fraction_ref[...]
    bracket = jnp.zeros((outputs, tiles), jnp.int32)
    for s in range(1, sections):
        bracket = bracket + (depths[s] <= target).astype(jnp.int32)
    bracket = jnp.minimum(bracket, sections - 2)
    lower = jnp.zeros((outputs, tiles), jnp.float32)
    upper = jnp.zeros((outputs, tiles), jnp.float32)
    for s in range(sections - 1):
        here = bracket == s
        lower = jnp.where(here, depths[s], lower)
        upper = jnp.where(here, depths[s + 1], upper)
    lifted = bracket.astype(jnp.float32) + (target - lower) / (upper - lower)
    beyond = lifted - bracket.astype(jnp.float32)
    pair = jnp.concatenate(
        [1.0 - jnp.abs(beyond), jnp.maximum(0.0, 1.0 - jnp.abs(beyond - 1.0))], axis=0
    )
    used = lax.broadcasted_iota(jnp.int32, pair.shape, 1) % 4 == 0
    spread_ref[...] = jnp.dot(
        jnp.where(used, jnp.maximum(0.0, pair), 0.0).astype(jnp.bfloat16),
        to_pixels_ref[...],
        preferred_element_type=jnp.float32,
    )
    first = lax.broadcasted_iota(jnp.int32, (rows, LANES), 1) < TILE

    def to_hbm(j):
        some = pl.ds(2 * j, 2)
        return pltpu.make_async_copy(
            made_ref.at[some], out_ref.at[some], out_sems.at[j]
        )

    for j in range(outputs):
        made = []
        for g in range(cols // LANES):
            lanes = pl.ds(g * LANES, LANES)
            ahead = x_ref[pl.ds(bracket[j, lane_of_tile(2 * g)], 2), :, lanes]
            behind = x_ref[pl.ds(bracket[j, lane_of_tile(2 * g + 1)], 2), :, lanes]
            near = jnp.where(first, ahead[0], behind[0])
            far = jnp.where(first, ahead[1], behind[1])
            made.append(
                (
                    spread_ref[j : j + 1, lanes] * near.astype(jnp.float32)
                    + spread_ref[outputs + j : outputs + j + 1, lanes]
                    * far.astype(jnp.float32)
                ).astype(jnp.bfloat16)
            )
        for g, values in enumerate(made):
            made_ref[j, :, g * LANES : (g + 1) * LANES] = values
        if j % 2:
            to_hbm(j // 2).start()
    for j in range(outputs // 2):
        to_hbm(j).wait()


def per_device(sections, calibration_knots, target_offset, target_step):
    section_total = lax.axis_size("sec")
    position = lax.axis_index("sec")
    row_total, cols = sections.shape[1:]
    rows_local = row_total // section_total
    sharers = TILE // rows_local
    tiles = cols // TILE
    if rows_local % 16 or section_total != 16 or tiles * 4 != LANES or sharers > 16:
        return plain_per_device(
            sections, calibration_knots, target_offset, target_step
        )
    blocks = sections.reshape(section_total, rows_local, cols)
    pencils = lax.all_to_all(blocks, "sec", split_axis=0, concat_axis=0, tiled=True)
    height = 8 * (AHEAD + 2) // 2
    vmem = pl.BlockSpec(memory_space=pltpu.VMEM)
    smem = pl.BlockSpec(memory_space=pltpu.SMEM)
    pixels = section_total * rows_local * cols
    tile_row = (position * rows_local // TILE).astype(jnp.int32).reshape(1)
    pairing, to_pixels, fraction, curve = pl.pallas_call(
        tables_kernel,
        out_shape=[
            jax.ShapeDtypeStruct((2 * LANES, LANES), jnp.bfloat16),
            jax.ShapeDtypeStruct((LANES, cols), jnp.bfloat16),
            jax.ShapeDtypeStruct((section_total, LANES), jnp.float32),
            jax.ShapeDtypeStruct((calibration_knots.shape[0], LANES), jnp.float32),
        ],
        in_specs=[smem, smem, vmem, vmem],
        out_specs=[vmem] * 4,
        compiler_params=pltpu.CompilerParams(vmem_limit_bytes=4 * 2**20),
        cost_estimate=pl.CostEstimate(
            flops=2**20, bytes_accessed=2**20, transcendentals=0
        ),
    )(tile_row, calibration_knots, target_offset, target_step)
    partial_sums = pl.pallas_call(
        sums_kernel,
        out_shape=jax.ShapeDtypeStruct((height, LANES), jnp.float32),
        in_specs=[vmem] * 2,
        out_specs=vmem,
        scratch_shapes=[
            pltpu.VMEM(
                (cols // 2 // LANES, section_total * 17, LANES), jnp.float32
            ),
            pltpu.VMEM(
                (cols // 2 // LANES, rows_local // 2, section_total + 8, LANES),
                jnp.float32,
            ),
        ],
        compiler_params=pltpu.CompilerParams(vmem_limit_bytes=16 * 2**20),
        cost_estimate=pl.CostEstimate(
            flops=pixels * 8, bytes_accessed=pixels * 2, transcendentals=0
        ),
    )(pencils, pairing)
    all_sums = [partial_sums]
    for other in range(1, sharers):
        all_sums.append(
            lax.ppermute(
                partial_sums, "sec", [(i, i ^ other) for i in range(section_total)]
            )
        )
    return pl.pallas_call(
        resample_kernel,
        out_shape=jax.ShapeDtypeStruct(pencils.shape, jnp.bfloat16),
        in_specs=[vmem] * (sharers + 4),
        out_specs=pl.BlockSpec(memory_space=pl.ANY),
        scratch_shapes=[
            pltpu.VMEM((2 * section_total, cols), jnp.float32),
            pltpu.VMEM(pencils.shape, jnp.bfloat16),
            pltpu.SemaphoreType.DMA((section_total // 2,)),
        ],
        compiler_params=pltpu.CompilerParams(vmem_limit_bytes=16 * 2**20),
        cost_estimate=pl.CostEstimate(
            flops=pixels * 2 * section_total, bytes_accessed=pixels * 4, transcendentals=0
        ),
    )(fraction, curve, to_pixels, *all_sums, pencils)


def solution(mesh):
    return jax.shard_map(
        per_device,
        mesh=mesh,
        in_specs=(P("sec", None, "tile"), P(), P(None, "tile"), P(None, "tile")),
        out_specs=P(None, "sec", "tile"),
        check_vma=False,
    )
```

```python
import functools

import jax
import jax.numpy as jnp
from jax import lax
from jax.experimental import pallas as pl
from jax.experimental.pallas import tpu as pltpu
from jax.sharding import PartitionSpec as P

TILE = 64
AHEAD = 4
LANES = 128
EPSILON = 1e-06


def from_behind(value, axis, steps):
    count = lax.axis_size(axis)
    first, last = (max(0, -steps), min(count, count - steps))
    return lax.ppermute(value, axis, [(source, source + steps) for source in range(first, last)])


def shrink(pixels):
    leading = pixels.shape[:-2]
    row_total = pixels.shape[-2]
    col_total = pixels.shape[-1]
    blocks = pixels.astype(jnp.float32).reshape(leading + (row_total // 2, 2, col_total // 2, 2))
    return jnp.mean(blocks, axis=(-3, -1)).astype(jnp.bfloat16)


def moments(current, following, row_group, half_tile):
    leading = current.shape[:-2]
    tiled_shape = leading + (
        current.shape[-2] // row_group,
        row_group,
        current.shape[-1] // half_tile,
        half_tile,
    )
    first_tile = current.astype(jnp.float32).reshape(tiled_shape)
    second_tile = following.astype(jnp.float32).reshape(tiled_shape)

    def tile_total(values):
        return jnp.sum(values, axis=(-3, -1))

    return (
        tile_total(first_tile),
        tile_total(second_tile),
        tile_total(first_tile * first_tile),
        tile_total(second_tile * second_tile),
        tile_total(first_tile * second_tile),
    )


def correlate(moment_sums, samples):
    sum_first, sum_second, sum_ff, sum_ss, sum_fs = moment_sums
    mean_first = sum_first / samples
    mean_second = sum_second / samples
    covariance = sum_fs / samples - mean_first * mean_second
    var_first = sum_ff / samples - mean_first * mean_first
    var_second = sum_ss / samples - mean_second * mean_second
    return covariance / jnp.sqrt(var_first * var_second + EPSILON)


def calibrate(correlation, knot_values):
    knot_total = knot_values.shape[0]
    knot_grid = -1.0 + jnp.arange(knot_total, dtype=jnp.float32) * (2.0 / (knot_total - 1))
    hat_weights = jnp.maximum(
        0.0, 1.0 - jnp.abs(correlation[..., None] - knot_grid) * ((knot_total - 1) / 2.0)
    )
    return jnp.sum(hat_weights * (knot_values.astype(jnp.float32) / 1000.0), axis=-1)


def exclusive_last(values):
    running = jnp.cumsum(values, axis=-1)
    return jnp.concatenate(
        [jnp.zeros(values.shape[:-1] + (1,), jnp.float32), running[..., :-1]], axis=-1
    )


def resample_weights(depths, offsets, strides, outputs):
    section_total = depths.shape[-1]
    grid_index = jnp.arange(outputs, dtype=jnp.int32)
    fraction = (offsets[..., None] + grid_index * strides[..., None]).astype(jnp.float32) / (
        64.0 * outputs
    )
    target = depths[..., -1:] * fraction
    bracket = jnp.sum((depths[..., None, 1:] <= target[..., None]).astype(jnp.int32), axis=-1)
    bracket = jnp.minimum(bracket, section_total - 2)
    section_places = jnp.arange(section_total, dtype=jnp.int32)
    lower_depth = jnp.sum(
        jnp.where(section_places == bracket[..., None], depths[..., None, :], 0.0), axis=-1
    )
    upper_depth = jnp.sum(
        jnp.where(section_places == bracket[..., None] + 1, depths[..., None, :], 0.0), axis=-1
    )
    lifted = bracket.astype(jnp.float32) + (target - lower_depth) / (upper_depth - lower_depth)
    spread = jnp.abs(lifted[..., None] - section_places.astype(jnp.float32))
    return jnp.maximum(0.0, 1.0 - spread).astype(jnp.bfloat16)


def plain_per_device(sections, calibration_knots, target_offset, target_step):
    section_total = lax.axis_size("sec")
    position = lax.axis_index("sec")
    half_tile = TILE // 2
    samples = float(half_tile * half_tile)
    row_total = sections.shape[1]
    rows_local = row_total // section_total
    tile_rows = row_total // TILE
    tiles_wide = sections.shape[2] // TILE
    tile_row = position * rows_local // TILE
    pencils = lax.all_to_all(sections, "sec", split_axis=1, concat_axis=0, tiled=True)
    reduced = shrink(sections[0])
    numerator = jnp.zeros((tile_rows, tiles_wide), jnp.float32)
    denominator = jnp.zeros((), jnp.float32)
    for spacing in range(1, AHEAD + 1):
        forward = from_behind(reduced, "sec", -spacing)
        correlation = correlate(moments(reduced, forward, half_tile, half_tile), samples)
        usable = (position + spacing < section_total).astype(jnp.float32)
        numerator = numerator + usable * (spacing * calibrate(correlation, calibration_knots))
        denominator = denominator + usable * float(spacing * spacing)
    thickness = numerator / jnp.maximum(denominator, 1.0)
    spread_rows = jnp.repeat(thickness, TILE, axis=0)[None]
    carried_maps = lax.all_to_all(spread_rows, "sec", split_axis=1, concat_axis=0, tiled=True)
    column_maps = jnp.transpose(carried_maps[:, 0, :])
    depths = exclusive_last(column_maps)
    offsets_row = lax.dynamic_index_in_dim(target_offset, tile_row, 0, keepdims=False)
    strides_row = lax.dynamic_index_in_dim(target_step, tile_row, 0, keepdims=False)
    weights = resample_weights(depths, offsets_row, strides_row, section_total)
    pencil_tiles = pencils.reshape(section_total, rows_local, tiles_wide, TILE)
    resampled = jnp.einsum(
        "tjs,srtc->jrtc", weights, pencil_tiles, preferred_element_type=jnp.float32
    )
    return resampled.reshape(section_total, rows_local, sections.shape[2]).astype(jnp.bfloat16)


def one_hot(shape, row_of, col_of):
    rows = lax.broadcasted_iota(jnp.int32, shape, 0)
    cols = lax.broadcasted_iota(jnp.int32, shape, 1)
    return (row_of(rows) == col_of(cols)).astype(jnp.float32).astype(jnp.bfloat16)


def shift_up(values, steps):
    if steps == 0:
        return values
    return jnp.concatenate([values[steps:], jnp.zeros_like(values[:steps])], axis=0)


def tile_of_lane(lanes):
    group = (lanes // 16) % 2 + 2 * ((lanes // 8) % 2) + 4 * ((lanes // 4) % 2)
    return lanes // 32 + 4 * group


def lane_of_tile(tile):
    group = tile // 4
    return 32 * (tile % 4) + 16 * (group % 2) + 8 * (group // 2 % 2) + 4 * (group // 4)


def tables_kernel(
    tile_row_ref,
    knots_ref,
    offset_ref,
    step_ref,
    pairing_ref,
    to_pixels_ref,
    fraction_ref,
    curve_ref,
):
    pairing_ref[...] = one_hot(pairing_ref.shape, lambda r: r // 2, lambda c: c)
    to_pixels_ref[...] = one_hot(
        to_pixels_ref.shape,
        lambda r: jnp.where(r % 4 == 0, tile_of_lane(r), -1),
        lambda c: c // TILE,
    )
    outputs = fraction_ref.shape[0]
    row = tile_row_ref[0]
    to_lanes = one_hot(
        (offset_ref.shape[1], LANES), lambda r: r, lambda c: tile_of_lane(c)
    )

    def spread(ref):
        values = jnp.broadcast_to(ref[pl.ds(row, 1), :], (16, ref.shape[1]))
        return jnp.dot(
            values.astype(jnp.float32).astype(jnp.bfloat16),
            to_lanes,
            preferred_element_type=jnp.float32,
        )[:1]

    index = lax.broadcasted_iota(jnp.int32, fraction_ref.shape, 0).astype(jnp.float32)
    fraction_ref[...] = (spread(offset_ref) + index * spread(step_ref)) / (
        64.0 * outputs
    )
    for j in range(curve_ref.shape[0]):
        curve_ref[pl.ds(j, 1), :] = jnp.full(
            (1, curve_ref.shape[1]), knots_ref[j].astype(jnp.float32) / 1000.0
        )


def fold(first, second, width, lanes):
    return jnp.where(
        (lanes // width) % 2 == 0,
        first + pltpu.roll(first, LANES - width, 1),
        second + pltpu.roll(second, width, 1),
    )


def sums_kernel(x_ref, pairing_ref, sums_ref, pairs_ref, reduced_ref):
    sections, rows, cols = x_ref.shape
    groups = cols // 2 // LANES
    pairing = pairing_ref[...]
    for g in range(groups):
        wide = x_ref[:, :, 2 * LANES * g : 2 * LANES * (g + 1)]
        pairs = jnp.dot(
            wide.reshape(sections * rows, 2 * LANES),
            pairing,
            preferred_element_type=jnp.float32,
        )
        for s in range(sections):
            pairs_ref[g, pl.ds(17 * s, rows), :] = pairs[rows * s : rows * (s + 1)]
    lanes = lax.broadcasted_iota(jnp.int32, (sections, LANES), 1)
    waiting = {}
    for g in range(groups):
        total = [jnp.zeros((sections, LANES), jnp.float32)] * (AHEAD + 2)
        for r in range(rows // 2):
            upper = pairs_ref[g, pl.ds(2 * r, sections, stride=17), :]
            lower = pairs_ref[g, pl.ds(2 * r + 1, sections, stride=17), :]
            reduced = ((upper + lower) * 0.25).astype(jnp.bfloat16).astype(jnp.float32)
            reduced_ref[g, r, :sections] = reduced
            reduced_ref[g, r, sections:] = jnp.zeros((8, LANES), jnp.float32)
            total[0] = total[0] + reduced
            total[1] = total[1] + reduced * reduced
            for k in range(1, AHEAD + 1):
                total[k + 1] = total[k + 1] + reduced * reduced_ref[g, r, k : k + sections]
        width = 16
        while (g * width // 16) % 2 == 1 and width >= 4:
            total = [fold(a, b, width, lanes) for a, b in zip(waiting.pop(width), total)]
            width //= 2
        waiting[width] = total
    total = waiting.pop(2)
    for v in range((AHEAD + 2) // 2):
        pair = fold(total[2 * v], total[2 * v + 1], 2, lanes)
        sums_ref[8 * v : 8 * v + 8] = fold(pair[:8], pair[8:], 1, lanes[:8])


def tree_sum(values):
    while len(values) > 1:
        rest = values[len(values) // 2 * 2 :]
        values = [x + y for x, y in zip(values[::2], values[1::2])] + rest
    return values[0]


def resample_kernel(fraction_ref, curve_ref, to_pixels_ref, *refs):
    *sums_refs, x_ref, out_ref, spread_ref, made_ref, out_sems = refs
    sections, rows, cols = x_ref.shape
    outputs = out_ref.shape[0]
    tiles = LANES
    samples = float((TILE // 2) ** 2)
    packed = sums_refs[0][...]
    for ref in sums_refs[1:]:
        packed = packed + ref[...]

    def unpack(q, half):
        part = packed[8 * (q // 2) : 8 * (q // 2) + 8]
        b = 2 * (q % 2) + half
        return pltpu.roll(part, LANES - b, 1) if b else part

    quantity = [
        jnp.concatenate([unpack(q, 0), unpack(q, 1)], axis=0) for q in range(AHEAD + 2)
    ]
    mean = quantity[0] / samples
    variance = quantity[1] / samples - mean * mean
    place = lax.broadcasted_iota(jnp.int32, (sections, tiles), 0)
    numerator = jnp.zeros((sections, tiles), jnp.float32)
    denominator = jnp.zeros((sections, tiles), jnp.float32)
    knots = curve_ref.shape[0]
    for k in range(1, AHEAD + 1):
        covariance = quantity[k + 1] / samples - mean * shift_up(mean, k)
        correlation = covariance / jnp.sqrt(variance * shift_up(variance, k) + EPSILON)
        scaled = correlation * ((knots - 1) / 2.0)
        distance = tree_sum(
            [
                jnp.maximum(0.0, 1.0 - jnp.abs(scaled - (j - (knots - 1) / 2.0)))
                * curve_ref[j : j + 1, :]
                for j in range(knots)
            ]
        )
        usable = (place + k < sections).astype(jnp.float32)
        numerator = numerator + usable * (k * distance)
        denominator = denominator + usable * float(k * k)
    thickness = numerator / jnp.maximum(denominator, 1.0)
    depths = [jnp.zeros((1, tiles), jnp.float32)]
    for s in range(sections - 1):
        depths.append(depths[-1] + thickness[s : s + 1])
    target = depths[-1] * fraction_ref[...]
    bracket = tree_sum(
        [(depths[s] <= target).astype(jnp.int32) for s in range(1, sections)]
    )
    bracket = jnp.minimum(bracket, sections - 2)
    here = [bracket == s for s in range(sections - 1)]
    lower = tree_sum([jnp.where(h, depths[s], 0.0) for s, h in enumerate(here)])
    upper = tree_sum([jnp.where(h, depths[s + 1], 0.0) for s, h in enumerate(here)])
    lifted = bracket.astype(jnp.float32) + (target - lower) / (upper - lower)
    beyond = lifted - bracket.astype(jnp.float32)
    pair = jnp.concatenate(
        [1.0 - jnp.abs(beyond), jnp.maximum(0.0, 1.0 - jnp.abs(beyond - 1.0))], axis=0
    )
    used = lax.broadcasted_iota(jnp.int32, pair.shape, 1) % 4 == 0
    spread_ref[...] = jnp.dot(
        jnp.where(used, jnp.maximum(0.0, pair), 0.0).astype(jnp.bfloat16),
        to_pixels_ref[...],
        preferred_element_type=jnp.float32,
    )
    first = lax.broadcasted_iota(jnp.int32, (rows, LANES), 1) < TILE

    def to_hbm(j):
        some = pl.ds(2 * j, 2)
        return pltpu.make_async_copy(
            made_ref.at[some], out_ref.at[some], out_sems.at[j]
        )

    for j in range(outputs):
        made = []
        for g in range(cols // LANES):
            lanes = pl.ds(g * LANES, LANES)
            ahead = x_ref[pl.ds(bracket[j, lane_of_tile(2 * g)], 2), :, lanes]
            behind = x_ref[pl.ds(bracket[j, lane_of_tile(2 * g + 1)], 2), :, lanes]
            near = jnp.where(first, ahead[0], behind[0])
            far = jnp.where(first, ahead[1], behind[1])
            made.append(
                (
                    spread_ref[j : j + 1, lanes] * near.astype(jnp.float32)
                    + spread_ref[outputs + j : outputs + j + 1, lanes]
                    * far.astype(jnp.float32)
                ).astype(jnp.bfloat16)
            )
        for g, values in enumerate(made):
            made_ref[j, :, g * LANES : (g + 1) * LANES] = values
        if j % 2:
            to_hbm(j // 2).start()
    for j in range(outputs // 2):
        to_hbm(j).wait()


def per_device(sections, calibration_knots, target_offset, target_step):
    section_total = lax.axis_size("sec")
    position = lax.axis_index("sec")
    row_total, cols = sections.shape[1:]
    rows_local = row_total // section_total
    sharers = TILE // rows_local
    tiles = cols // TILE
    if rows_local % 16 or section_total != 16 or tiles * 4 != LANES or sharers > 16:
        return plain_per_device(
            sections, calibration_knots, target_offset, target_step
        )
    blocks = sections.reshape(section_total, rows_local, cols)
    pencils = lax.all_to_all(blocks, "sec", split_axis=0, concat_axis=0, tiled=True)
    height = 8 * (AHEAD + 2) // 2
    vmem = pl.BlockSpec(memory_space=pltpu.VMEM)
    smem = pl.BlockSpec(memory_space=pltpu.SMEM)
    pixels = section_total * rows_local * cols
    tile_row = (position * rows_local // TILE).astype(jnp.int32).reshape(1)
    pairing, to_pixels, fraction, curve = pl.pallas_call(
        tables_kernel,
        out_shape=[
            jax.ShapeDtypeStruct((2 * LANES, LANES), jnp.bfloat16),
            jax.ShapeDtypeStruct((LANES, cols), jnp.bfloat16),
            jax.ShapeDtypeStruct((section_total, LANES), jnp.float32),
            jax.ShapeDtypeStruct((calibration_knots.shape[0], LANES), jnp.float32),
        ],
        in_specs=[smem, smem, vmem, vmem],
        out_specs=[vmem] * 4,
        compiler_params=pltpu.CompilerParams(vmem_limit_bytes=4 * 2**20),
        cost_estimate=pl.CostEstimate(
            flops=2**20, bytes_accessed=2**20, transcendentals=0
        ),
    )(tile_row, calibration_knots, target_offset, target_step)
    partial_sums = pl.pallas_call(
        sums_kernel,
        out_shape=jax.ShapeDtypeStruct((height, LANES), jnp.float32),
        in_specs=[vmem] * 2,
        out_specs=vmem,
        scratch_shapes=[
            pltpu.VMEM(
                (cols // 2 // LANES, section_total * 17, LANES), jnp.float32
            ),
            pltpu.VMEM(
                (cols // 2 // LANES, rows_local // 2, section_total + 8, LANES),
                jnp.float32,
            ),
        ],
        compiler_params=pltpu.CompilerParams(vmem_limit_bytes=16 * 2**20),
        cost_estimate=pl.CostEstimate(
            flops=pixels * 8, bytes_accessed=pixels * 2, transcendentals=0
        ),
    )(pencils, pairing)
    all_sums = [partial_sums]
    for other in range(1, sharers):
        all_sums.append(
            lax.ppermute(
                partial_sums, "sec", [(i, i ^ other) for i in range(section_total)]
            )
        )
    return pl.pallas_call(
        resample_kernel,
        out_shape=jax.ShapeDtypeStruct(pencils.shape, jnp.bfloat16),
        in_specs=[vmem] * (sharers + 4),
        out_specs=pl.BlockSpec(memory_space=pl.ANY),
        scratch_shapes=[
            pltpu.VMEM((2 * section_total, cols), jnp.float32),
            pltpu.VMEM(pencils.shape, jnp.bfloat16),
            pltpu.SemaphoreType.DMA((section_total // 2,)),
        ],
        compiler_params=pltpu.CompilerParams(vmem_limit_bytes=16 * 2**20),
        cost_estimate=pl.CostEstimate(
            flops=pixels * 2 * section_total, bytes_accessed=pixels * 4, transcendentals=0
        ),
    )(fraction, curve, to_pixels, *all_sums, pencils)


def solution(mesh):
    return jax.shard_map(
        per_device,
        mesh=mesh,
        in_specs=(P("sec", None, "tile"), P(), P(None, "tile"), P(None, "tile")),
        out_specs=P(None, "sec", "tile"),
        check_vma=False,
    )
```

```python
import functools

import jax
import jax.numpy as jnp
from jax import lax
from jax.experimental import pallas as pl
from jax.experimental.pallas import tpu as pltpu
from jax.sharding import PartitionSpec as P

TILE = 64
AHEAD = 4
LANES = 128
EPSILON = 1e-06


def from_behind(value, axis, steps):
    count = lax.axis_size(axis)
    first, last = (max(0, -steps), min(count, count - steps))
    return lax.ppermute(value, axis, [(source, source + steps) for source in range(first, last)])


def shrink(pixels):
    leading = pixels.shape[:-2]
    row_total = pixels.shape[-2]
    col_total = pixels.shape[-1]
    blocks = pixels.astype(jnp.float32).reshape(leading + (row_total // 2, 2, col_total // 2, 2))
    return jnp.mean(blocks, axis=(-3, -1)).astype(jnp.bfloat16)


def moments(current, following, row_group, half_tile):
    leading = current.shape[:-2]
    tiled_shape = leading + (
        current.shape[-2] // row_group,
        row_group,
        current.shape[-1] // half_tile,
        half_tile,
    )
    first_tile = current.astype(jnp.float32).reshape(tiled_shape)
    second_tile = following.astype(jnp.float32).reshape(tiled_shape)

    def tile_total(values):
        return jnp.sum(values, axis=(-3, -1))

    return (
        tile_total(first_tile),
        tile_total(second_tile),
        tile_total(first_tile * first_tile),
        tile_total(second_tile * second_tile),
        tile_total(first_tile * second_tile),
    )


def correlate(moment_sums, samples):
    sum_first, sum_second, sum_ff, sum_ss, sum_fs = moment_sums
    mean_first = sum_first / samples
    mean_second = sum_second / samples
    covariance = sum_fs / samples - mean_first * mean_second
    var_first = sum_ff / samples - mean_first * mean_first
    var_second = sum_ss / samples - mean_second * mean_second
    return covariance / jnp.sqrt(var_first * var_second + EPSILON)


def calibrate(correlation, knot_values):
    knot_total = knot_values.shape[0]
    knot_grid = -1.0 + jnp.arange(knot_total, dtype=jnp.float32) * (2.0 / (knot_total - 1))
    hat_weights = jnp.maximum(
        0.0, 1.0 - jnp.abs(correlation[..., None] - knot_grid) * ((knot_total - 1) / 2.0)
    )
    return jnp.sum(hat_weights * (knot_values.astype(jnp.float32) / 1000.0), axis=-1)


def exclusive_last(values):
    running = jnp.cumsum(values, axis=-1)
    return jnp.concatenate(
        [jnp.zeros(values.shape[:-1] + (1,), jnp.float32), running[..., :-1]], axis=-1
    )


def resample_weights(depths, offsets, strides, outputs):
    section_total = depths.shape[-1]
    grid_index = jnp.arange(outputs, dtype=jnp.int32)
    fraction = (offsets[..., None] + grid_index * strides[..., None]).astype(jnp.float32) / (
        64.0 * outputs
    )
    target = depths[..., -1:] * fraction
    bracket = jnp.sum((depths[..., None, 1:] <= target[..., None]).astype(jnp.int32), axis=-1)
    bracket = jnp.minimum(bracket, section_total - 2)
    section_places = jnp.arange(section_total, dtype=jnp.int32)
    lower_depth = jnp.sum(
        jnp.where(section_places == bracket[..., None], depths[..., None, :], 0.0), axis=-1
    )
    upper_depth = jnp.sum(
        jnp.where(section_places == bracket[..., None] + 1, depths[..., None, :], 0.0), axis=-1
    )
    lifted = bracket.astype(jnp.float32) + (target - lower_depth) / (upper_depth - lower_depth)
    spread = jnp.abs(lifted[..., None] - section_places.astype(jnp.float32))
    return jnp.maximum(0.0, 1.0 - spread).astype(jnp.bfloat16)


def plain_per_device(sections, calibration_knots, target_offset, target_step):
    section_total = lax.axis_size("sec")
    position = lax.axis_index("sec")
    half_tile = TILE // 2
    samples = float(half_tile * half_tile)
    row_total = sections.shape[1]
    rows_local = row_total // section_total
    tile_rows = row_total // TILE
    tiles_wide = sections.shape[2] // TILE
    tile_row = position * rows_local // TILE
    pencils = lax.all_to_all(sections, "sec", split_axis=1, concat_axis=0, tiled=True)
    reduced = shrink(sections[0])
    numerator = jnp.zeros((tile_rows, tiles_wide), jnp.float32)
    denominator = jnp.zeros((), jnp.float32)
    for spacing in range(1, AHEAD + 1):
        forward = from_behind(reduced, "sec", -spacing)
        correlation = correlate(moments(reduced, forward, half_tile, half_tile), samples)
        usable = (position + spacing < section_total).astype(jnp.float32)
        numerator = numerator + usable * (spacing * calibrate(correlation, calibration_knots))
        denominator = denominator + usable * float(spacing * spacing)
    thickness = numerator / jnp.maximum(denominator, 1.0)
    spread_rows = jnp.repeat(thickness, TILE, axis=0)[None]
    carried_maps = lax.all_to_all(spread_rows, "sec", split_axis=1, concat_axis=0, tiled=True)
    column_maps = jnp.transpose(carried_maps[:, 0, :])
    depths = exclusive_last(column_maps)
    offsets_row = lax.dynamic_index_in_dim(target_offset, tile_row, 0, keepdims=False)
    strides_row = lax.dynamic_index_in_dim(target_step, tile_row, 0, keepdims=False)
    weights = resample_weights(depths, offsets_row, strides_row, section_total)
    pencil_tiles = pencils.reshape(section_total, rows_local, tiles_wide, TILE)
    resampled = jnp.einsum(
        "tjs,srtc->jrtc", weights, pencil_tiles, preferred_element_type=jnp.float32
    )
    return resampled.reshape(section_total, rows_local, sections.shape[2]).astype(jnp.bfloat16)


def one_hot(shape, row_of, col_of):
    rows = lax.broadcasted_iota(jnp.int32, shape, 0)
    cols = lax.broadcasted_iota(jnp.int32, shape, 1)
    return (row_of(rows) == col_of(cols)).astype(jnp.float32).astype(jnp.bfloat16)


def shift_up(values, steps):
    if steps == 0:
        return values
    return jnp.concatenate([values[steps:], jnp.zeros_like(values[:steps])], axis=0)


def tile_of_lane(lanes):
    group = (lanes // 16) % 2 + 2 * ((lanes // 8) % 2) + 4 * ((lanes // 4) % 2)
    return lanes // 32 + 4 * group


def lane_of_tile(tile):
    group = tile // 4
    return 32 * (tile % 4) + 16 * (group % 2) + 8 * (group // 2 % 2) + 4 * (group // 4)


def tables_kernel(
    tile_row_ref,
    knots_ref,
    offset_ref,
    step_ref,
    pairing_ref,
    to_pixels_ref,
    fraction_ref,
    curve_ref,
):
    pairing_ref[...] = 0.25 * one_hot(pairing_ref.shape, lambda r: r // 2, lambda c: c)
    to_pixels_ref[...] = one_hot(
        to_pixels_ref.shape,
        lambda r: jnp.where(r % 4 == 0, tile_of_lane(r), -1),
        lambda c: c // TILE,
    )
    outputs = fraction_ref.shape[0]
    row = tile_row_ref[0]
    to_lanes = one_hot(
        (offset_ref.shape[1], LANES), lambda r: r, lambda c: tile_of_lane(c)
    )

    def spread(ref):
        values = jnp.broadcast_to(ref[pl.ds(row, 1), :], (16, ref.shape[1]))
        return jnp.dot(
            values.astype(jnp.float32).astype(jnp.bfloat16),
            to_lanes,
            preferred_element_type=jnp.float32,
        )[:1]

    index = lax.broadcasted_iota(jnp.int32, fraction_ref.shape, 0).astype(jnp.float32)
    fraction_ref[...] = (spread(offset_ref) + index * spread(step_ref)) / (
        64.0 * outputs
    )
    for j in range(curve_ref.shape[0]):
        curve_ref[pl.ds(j, 1), :] = jnp.full(
            (1, curve_ref.shape[1]), knots_ref[j].astype(jnp.float32) / 1000.0
        )


def fold(first, second, width, lanes):
    return jnp.where(
        (lanes // width) % 2 == 0,
        first + pltpu.roll(first, LANES - width, 1),
        second + pltpu.roll(second, width, 1),
    )


def sums_kernel(x_ref, pairing_ref, sums_ref, pairs_ref, reduced_ref):
    sections, rows, cols = x_ref.shape
    groups = cols // 2 // LANES
    pairing = pairing_ref[...]
    for g in range(groups):
        wide = x_ref[:, :, 2 * LANES * g : 2 * LANES * (g + 1)]
        pairs = jnp.dot(
            wide.reshape(sections * rows, 2 * LANES),
            pairing,
            preferred_element_type=jnp.float32,
        )
        for s in range(sections):
            pairs_ref[g, pl.ds(17 * s, rows), :] = pairs[rows * s : rows * (s + 1)]
    lanes = lax.broadcasted_iota(jnp.int32, (sections, LANES), 1)
    waiting = {}
    for g in range(groups):
        total = [jnp.zeros((sections, LANES), jnp.float32)] * (AHEAD + 2)
        for r in range(rows // 2):
            upper = pairs_ref[g, pl.ds(2 * r, sections, stride=17), :]
            lower = pairs_ref[g, pl.ds(2 * r + 1, sections, stride=17), :]
            reduced = (upper + lower).astype(jnp.bfloat16).astype(jnp.float32)
            reduced_ref[g, r, :sections] = reduced
            reduced_ref[g, r, sections:] = jnp.zeros((8, LANES), jnp.float32)
            total[0] = total[0] + reduced
            total[1] = total[1] + reduced * reduced
            for k in range(1, AHEAD + 1):
                total[k + 1] = total[k + 1] + reduced * reduced_ref[g, r, k : k + sections]
        width = 16
        while (g * width // 16) % 2 == 1 and width >= 4:
            total = [fold(a, b, width, lanes) for a, b in zip(waiting.pop(width), total)]
            width //= 2
        waiting[width] = total
    total = waiting.pop(2)
    for v in range((AHEAD + 2) // 2):
        pair = fold(total[2 * v], total[2 * v + 1], 2, lanes)
        sums_ref[8 * v : 8 * v + 8] = fold(pair[:8], pair[8:], 1, lanes[:8])


def tree_sum(values):
    while len(values) > 1:
        rest = values[len(values) // 2 * 2 :]
        values = [x + y for x, y in zip(values[::2], values[1::2])] + rest
    return values[0]


def resample_kernel(fraction_ref, curve_ref, to_pixels_ref, *refs):
    *sums_refs, x_ref, out_ref, spread_ref, made_ref, out_sems = refs
    sections, rows, cols = x_ref.shape
    outputs = out_ref.shape[0]
    tiles = LANES
    samples = float((TILE // 2) ** 2)
    packed = sums_refs[0][...]
    for ref in sums_refs[1:]:
        packed = packed + ref[...]

    def unpack(q, half):
        part = packed[8 * (q // 2) : 8 * (q // 2) + 8]
        b = 2 * (q % 2) + half
        return pltpu.roll(part, LANES - b, 1) if b else part

    quantity = [
        jnp.concatenate([unpack(q, 0), unpack(q, 1)], axis=0) for q in range(AHEAD + 2)
    ]
    mean = quantity[0] / samples
    variance = quantity[1] / samples - mean * mean
    place = lax.broadcasted_iota(jnp.int32, (sections, tiles), 0)
    numerator = jnp.zeros((sections, tiles), jnp.float32)
    denominator = jnp.zeros((sections, tiles), jnp.float32)
    knots = curve_ref.shape[0]
    for k in range(1, AHEAD + 1):
        covariance = quantity[k + 1] / samples - mean * shift_up(mean, k)
        correlation = covariance / jnp.sqrt(variance * shift_up(variance, k) + EPSILON)
        scaled = correlation * ((knots - 1) / 2.0)
        distance = tree_sum(
            [
                jnp.maximum(0.0, 1.0 - jnp.abs(scaled - (j - (knots - 1) / 2.0)))
                * curve_ref[j : j + 1, :]
                for j in range(knots)
            ]
        )
        usable = (place + k < sections).astype(jnp.float32)
        numerator = numerator + usable * (k * distance)
        denominator = denominator + usable * float(k * k)
    thickness = numerator / jnp.maximum(denominator, 1.0)
    depths = [jnp.zeros((1, tiles), jnp.float32)]
    for s in range(sections - 1):
        depths.append(depths[-1] + thickness[s : s + 1])
    target = depths[-1] * fraction_ref[...]
    bracket = tree_sum(
        [(depths[s] <= target).astype(jnp.int32) for s in range(1, sections)]
    )
    bracket = jnp.minimum(bracket, sections - 2)
    here = [bracket == s for s in range(sections - 1)]
    lower = tree_sum([jnp.where(h, depths[s], 0.0) for s, h in enumerate(here)])
    upper = tree_sum([jnp.where(h, depths[s + 1], 0.0) for s, h in enumerate(here)])
    lifted = bracket.astype(jnp.float32) + (target - lower) / (upper - lower)
    beyond = lifted - bracket.astype(jnp.float32)
    pair = jnp.concatenate(
        [1.0 - jnp.abs(beyond), jnp.maximum(0.0, 1.0 - jnp.abs(beyond - 1.0))], axis=0
    )
    used = lax.broadcasted_iota(jnp.int32, pair.shape, 1) % 4 == 0
    spread_ref[...] = jnp.dot(
        jnp.where(used, jnp.maximum(0.0, pair), 0.0).astype(jnp.bfloat16),
        to_pixels_ref[...],
        preferred_element_type=jnp.float32,
    )
    first = lax.broadcasted_iota(jnp.int32, (rows, LANES), 1) < TILE

    def to_hbm(j):
        some = pl.ds(2 * j, 2)
        return pltpu.make_async_copy(
            made_ref.at[some], out_ref.at[some], out_sems.at[j]
        )

    for j in range(outputs):
        made = []
        for g in range(cols // LANES):
            lanes = pl.ds(g * LANES, LANES)
            ahead = x_ref[pl.ds(bracket[j, lane_of_tile(2 * g)], 2), :, lanes]
            behind = x_ref[pl.ds(bracket[j, lane_of_tile(2 * g + 1)], 2), :, lanes]
            near = jnp.where(first, ahead[0], behind[0])
            far = jnp.where(first, ahead[1], behind[1])
            made.append(
                (
                    spread_ref[j : j + 1, lanes] * near.astype(jnp.float32)
                    + spread_ref[outputs + j : outputs + j + 1, lanes]
                    * far.astype(jnp.float32)
                ).astype(jnp.bfloat16)
            )
        for g, values in enumerate(made):
            made_ref[j, :, g * LANES : (g + 1) * LANES] = values
        if j % 2:
            to_hbm(j // 2).start()
    for j in range(outputs // 2):
        to_hbm(j).wait()


def per_device(sections, calibration_knots, target_offset, target_step):
    section_total = lax.axis_size("sec")
    position = lax.axis_index("sec")
    row_total, cols = sections.shape[1:]
    rows_local = row_total // section_total
    sharers = TILE // rows_local
    tiles = cols // TILE
    if rows_local % 16 or section_total != 16 or tiles * 4 != LANES or sharers > 16:
        return plain_per_device(
            sections, calibration_knots, target_offset, target_step
        )
    blocks = sections.reshape(section_total, rows_local, cols)
    pencils = lax.all_to_all(blocks, "sec", split_axis=0, concat_axis=0, tiled=True)
    height = 8 * (AHEAD + 2) // 2
    vmem = pl.BlockSpec(memory_space=pltpu.VMEM)
    smem = pl.BlockSpec(memory_space=pltpu.SMEM)
    pixels = section_total * rows_local * cols
    tile_row = (position * rows_local // TILE).astype(jnp.int32).reshape(1)
    pairing, to_pixels, fraction, curve = pl.pallas_call(
        tables_kernel,
        out_shape=[
            jax.ShapeDtypeStruct((2 * LANES, LANES), jnp.bfloat16),
            jax.ShapeDtypeStruct((LANES, cols), jnp.bfloat16),
            jax.ShapeDtypeStruct((section_total, LANES), jnp.float32),
            jax.ShapeDtypeStruct((calibration_knots.shape[0], LANES), jnp.float32),
        ],
        in_specs=[smem, smem, vmem, vmem],
        out_specs=[vmem] * 4,
        compiler_params=pltpu.CompilerParams(vmem_limit_bytes=4 * 2**20),
        cost_estimate=pl.CostEstimate(
            flops=2**20, bytes_accessed=2**20, transcendentals=0
        ),
    )(tile_row, calibration_knots, target_offset, target_step)
    partial_sums = pl.pallas_call(
        sums_kernel,
        out_shape=jax.ShapeDtypeStruct((height, LANES), jnp.float32),
        in_specs=[vmem] * 2,
        out_specs=vmem,
        scratch_shapes=[
            pltpu.VMEM(
                (cols // 2 // LANES, section_total * 17, LANES), jnp.float32
            ),
            pltpu.VMEM(
                (cols // 2 // LANES, rows_local // 2, section_total + 8, LANES),
                jnp.float32,
            ),
        ],
        compiler_params=pltpu.CompilerParams(vmem_limit_bytes=16 * 2**20),
        cost_estimate=pl.CostEstimate(
            flops=pixels * 8, bytes_accessed=pixels * 2, transcendentals=0
        ),
    )(pencils, pairing)
    all_sums = [partial_sums]
    for other in range(1, sharers):
        all_sums.append(
            lax.ppermute(
                partial_sums, "sec", [(i, i ^ other) for i in range(section_total)]
            )
        )
    return pl.pallas_call(
        resample_kernel,
        out_shape=jax.ShapeDtypeStruct(pencils.shape, jnp.bfloat16),
        in_specs=[vmem] * (sharers + 4),
        out_specs=pl.BlockSpec(memory_space=pl.ANY),
        scratch_shapes=[
            pltpu.VMEM((2 * section_total, cols), jnp.float32),
            pltpu.VMEM(pencils.shape, jnp.bfloat16),
            pltpu.SemaphoreType.DMA((section_total // 2,)),
        ],
        compiler_params=pltpu.CompilerParams(vmem_limit_bytes=16 * 2**20),
        cost_estimate=pl.CostEstimate(
            flops=pixels * 2 * section_total, bytes_accessed=pixels * 4, transcendentals=0
        ),
    )(fraction, curve, to_pixels, *all_sums, pencils)


def solution(mesh):
    return jax.shard_map(
        per_device,
        mesh=mesh,
        in_specs=(P("sec", None, "tile"), P(), P(None, "tile"), P(None, "tile")),
        out_specs=P(None, "sec", "tile"),
        check_vma=False,
    )
```

```python
import functools

import jax
import jax.numpy as jnp
from jax import lax
from jax.experimental import pallas as pl
from jax.experimental.pallas import tpu as pltpu
from jax.sharding import PartitionSpec as P

TILE = 64
AHEAD = 4
LANES = 128
EPSILON = 1e-06


def from_behind(value, axis, steps):
    count = lax.axis_size(axis)
    first, last = (max(0, -steps), min(count, count - steps))
    return lax.ppermute(value, axis, [(source, source + steps) for source in range(first, last)])


def shrink(pixels):
    leading = pixels.shape[:-2]
    row_total = pixels.shape[-2]
    col_total = pixels.shape[-1]
    blocks = pixels.astype(jnp.float32).reshape(leading + (row_total // 2, 2, col_total // 2, 2))
    return jnp.mean(blocks, axis=(-3, -1)).astype(jnp.bfloat16)


def moments(current, following, row_group, half_tile):
    leading = current.shape[:-2]
    tiled_shape = leading + (
        current.shape[-2] // row_group,
        row_group,
        current.shape[-1] // half_tile,
        half_tile,
    )
    first_tile = current.astype(jnp.float32).reshape(tiled_shape)
    second_tile = following.astype(jnp.float32).reshape(tiled_shape)

    def tile_total(values):
        return jnp.sum(values, axis=(-3, -1))

    return (
        tile_total(first_tile),
        tile_total(second_tile),
        tile_total(first_tile * first_tile),
        tile_total(second_tile * second_tile),
        tile_total(first_tile * second_tile),
    )


def correlate(moment_sums, samples):
    sum_first, sum_second, sum_ff, sum_ss, sum_fs = moment_sums
    mean_first = sum_first / samples
    mean_second = sum_second / samples
    covariance = sum_fs / samples - mean_first * mean_second
    var_first = sum_ff / samples - mean_first * mean_first
    var_second = sum_ss / samples - mean_second * mean_second
    return covariance / jnp.sqrt(var_first * var_second + EPSILON)


def calibrate(correlation, knot_values):
    knot_total = knot_values.shape[0]
    knot_grid = -1.0 + jnp.arange(knot_total, dtype=jnp.float32) * (2.0 / (knot_total - 1))
    hat_weights = jnp.maximum(
        0.0, 1.0 - jnp.abs(correlation[..., None] - knot_grid) * ((knot_total - 1) / 2.0)
    )
    return jnp.sum(hat_weights * (knot_values.astype(jnp.float32) / 1000.0), axis=-1)


def exclusive_last(values):
    running = jnp.cumsum(values, axis=-1)
    return jnp.concatenate(
        [jnp.zeros(values.shape[:-1] + (1,), jnp.float32), running[..., :-1]], axis=-1
    )


def resample_weights(depths, offsets, strides, outputs):
    section_total = depths.shape[-1]
    grid_index = jnp.arange(outputs, dtype=jnp.int32)
    fraction = (offsets[..., None] + grid_index * strides[..., None]).astype(jnp.float32) / (
        64.0 * outputs
    )
    target = depths[..., -1:] * fraction
    bracket = jnp.sum((depths[..., None, 1:] <= target[..., None]).astype(jnp.int32), axis=-1)
    bracket = jnp.minimum(bracket, section_total - 2)
    section_places = jnp.arange(section_total, dtype=jnp.int32)
    lower_depth = jnp.sum(
        jnp.where(section_places == bracket[..., None], depths[..., None, :], 0.0), axis=-1
    )
    upper_depth = jnp.sum(
        jnp.where(section_places == bracket[..., None] + 1, depths[..., None, :], 0.0), axis=-1
    )
    lifted = bracket.astype(jnp.float32) + (target - lower_depth) / (upper_depth - lower_depth)
    spread = jnp.abs(lifted[..., None] - section_places.astype(jnp.float32))
    return jnp.maximum(0.0, 1.0 - spread).astype(jnp.bfloat16)


def plain_per_device(sections, calibration_knots, target_offset, target_step):
    section_total = lax.axis_size("sec")
    position = lax.axis_index("sec")
    half_tile = TILE // 2
    samples = float(half_tile * half_tile)
    row_total = sections.shape[1]
    rows_local = row_total // section_total
    tile_rows = row_total // TILE
    tiles_wide = sections.shape[2] // TILE
    tile_row = position * rows_local // TILE
    pencils = lax.all_to_all(sections, "sec", split_axis=1, concat_axis=0, tiled=True)
    reduced = shrink(sections[0])
    numerator = jnp.zeros((tile_rows, tiles_wide), jnp.float32)
    denominator = jnp.zeros((), jnp.float32)
    for spacing in range(1, AHEAD + 1):
        forward = from_behind(reduced, "sec", -spacing)
        correlation = correlate(moments(reduced, forward, half_tile, half_tile), samples)
        usable = (position + spacing < section_total).astype(jnp.float32)
        numerator = numerator + usable * (spacing * calibrate(correlation, calibration_knots))
        denominator = denominator + usable * float(spacing * spacing)
    thickness = numerator / jnp.maximum(denominator, 1.0)
    spread_rows = jnp.repeat(thickness, TILE, axis=0)[None]
    carried_maps = lax.all_to_all(spread_rows, "sec", split_axis=1, concat_axis=0, tiled=True)
    column_maps = jnp.transpose(carried_maps[:, 0, :])
    depths = exclusive_last(column_maps)
    offsets_row = lax.dynamic_index_in_dim(target_offset, tile_row, 0, keepdims=False)
    strides_row = lax.dynamic_index_in_dim(target_step, tile_row, 0, keepdims=False)
    weights = resample_weights(depths, offsets_row, strides_row, section_total)
    pencil_tiles = pencils.reshape(section_total, rows_local, tiles_wide, TILE)
    resampled = jnp.einsum(
        "tjs,srtc->jrtc", weights, pencil_tiles, preferred_element_type=jnp.float32
    )
    return resampled.reshape(section_total, rows_local, sections.shape[2]).astype(jnp.bfloat16)


def one_hot(shape, row_of, col_of):
    rows = lax.broadcasted_iota(jnp.int32, shape, 0)
    cols = lax.broadcasted_iota(jnp.int32, shape, 1)
    return (row_of(rows) == col_of(cols)).astype(jnp.float32).astype(jnp.bfloat16)


def shift_up(values, steps):
    if steps == 0:
        return values
    return jnp.concatenate([values[steps:], jnp.zeros_like(values[:steps])], axis=0)


def tile_of_lane(lanes):
    group = (lanes // 16) % 2 + 2 * ((lanes // 8) % 2) + 4 * ((lanes // 4) % 2)
    return lanes // 32 + 4 * group


def lane_of_tile(tile):
    group = tile // 4
    return 32 * (tile % 4) + 16 * (group % 2) + 8 * (group // 2 % 2) + 4 * (group // 4)


def tables_kernel(
    tile_row_ref,
    knots_ref,
    offset_ref,
    step_ref,
    pairing_ref,
    to_pixels_ref,
    fraction_ref,
    curve_ref,
):
    pairing_ref[...] = 0.25 * one_hot(pairing_ref.shape, lambda r: r // 2, lambda c: c)
    to_pixels_ref[...] = one_hot(
        to_pixels_ref.shape,
        lambda r: jnp.where(r % 4 == 0, tile_of_lane(r), -1),
        lambda c: c // TILE,
    )
    outputs = fraction_ref.shape[0]
    row = tile_row_ref[0]
    to_lanes = one_hot(
        (offset_ref.shape[1], LANES), lambda r: r, lambda c: tile_of_lane(c)
    )

    def spread(ref):
        values = jnp.broadcast_to(ref[pl.ds(row, 1), :], (16, ref.shape[1]))
        return jnp.dot(
            values.astype(jnp.float32).astype(jnp.bfloat16),
            to_lanes,
            preferred_element_type=jnp.float32,
        )[:1]

    index = lax.broadcasted_iota(jnp.int32, fraction_ref.shape, 0).astype(jnp.float32)
    fraction_ref[...] = (spread(offset_ref) + index * spread(step_ref)) / (
        64.0 * outputs
    )
    for j in range(curve_ref.shape[0]):
        curve_ref[pl.ds(j, 1), :] = jnp.full(
            (1, curve_ref.shape[1]), knots_ref[j].astype(jnp.float32) / 1000.0
        )


def fold(first, second, width, lanes):
    return jnp.where(
        (lanes // width) % 2 == 0,
        first + pltpu.roll(first, LANES - width, 1),
        second + pltpu.roll(second, width, 1),
    )


def sums_kernel(x_ref, pairing_ref, sums_ref, pairs_ref, reduced_ref):
    sections, rows, cols = x_ref.shape
    groups = cols // 2 // LANES
    pairing = pairing_ref[...]
    for g in range(groups):
        wide = x_ref[:, :, 2 * LANES * g : 2 * LANES * (g + 1)]
        pairs = jnp.dot(
            wide.reshape(sections * rows, 2 * LANES),
            pairing,
            preferred_element_type=jnp.float32,
        )
        for s in range(sections):
            pairs_ref[g, pl.ds(17 * s, rows), :] = pairs[rows * s : rows * (s + 1)]
    lanes = lax.broadcasted_iota(jnp.int32, (sections, LANES), 1)
    waiting = {}
    for g in range(groups):
        total = [jnp.zeros((sections, LANES), jnp.float32)] * (AHEAD + 2)
        for r in range(rows // 2):
            upper = pairs_ref[g, pl.ds(2 * r, sections, stride=17), :]
            lower = pairs_ref[g, pl.ds(2 * r + 1, sections, stride=17), :]
            reduced = (upper + lower).astype(jnp.bfloat16).astype(jnp.float32)
            reduced_ref[g, r, :sections] = reduced
            reduced_ref[g, r, sections:] = jnp.zeros((8, LANES), jnp.float32)
            total[0] = total[0] + reduced
            total[1] = total[1] + reduced * reduced
            for k in range(1, AHEAD + 1):
                total[k + 1] = total[k + 1] + reduced * reduced_ref[g, r, k : k + sections]
        width = 16
        while (g * width // 16) % 2 == 1 and width >= 4:
            total = [fold(a, b, width, lanes) for a, b in zip(waiting.pop(width), total)]
            width //= 2
        waiting[width] = total
    total = waiting.pop(2)
    for v in range((AHEAD + 2) // 2):
        pair = fold(total[2 * v], total[2 * v + 1], 2, lanes)
        sums_ref[8 * v : 8 * v + 8] = fold(pair[:8], pair[8:], 1, lanes[:8])


def tree_sum(values):
    while len(values) > 1:
        rest = values[len(values) // 2 * 2 :]
        values = [x + y for x, y in zip(values[::2], values[1::2])] + rest
    return values[0]


def resample_kernel(fraction_ref, curve_ref, to_pixels_ref, *refs):
    *sums_refs, x_ref, out_ref, spread_ref, made_ref, out_sems = refs
    sections, rows, cols = x_ref.shape
    outputs = out_ref.shape[0]
    tiles = LANES
    share = 1.0 / float((TILE // 2) ** 2)
    packed = sums_refs[0][...]
    for ref in sums_refs[1:]:
        packed = packed + ref[...]

    def unpack(q, half):
        part = packed[8 * (q // 2) : 8 * (q // 2) + 8]
        b = 2 * (q % 2) + half
        return pltpu.roll(part, LANES - b, 1) if b else part

    quantity = [
        jnp.concatenate([unpack(q, 0), unpack(q, 1)], axis=0) for q in range(AHEAD + 2)
    ]
    mean = quantity[0] * share
    variance = quantity[1] * share - mean * mean
    place = lax.broadcasted_iota(jnp.int32, (sections, tiles), 0)
    numerator = jnp.zeros((sections, tiles), jnp.float32)
    denominator = jnp.zeros((sections, tiles), jnp.float32)
    knots = curve_ref.shape[0]
    for k in range(1, AHEAD + 1):
        covariance = quantity[k + 1] * share - mean * shift_up(mean, k)
        correlation = covariance / jnp.sqrt(variance * shift_up(variance, k) + EPSILON)
        scaled = correlation * ((knots - 1) / 2.0)
        distance = tree_sum(
            [
                jnp.maximum(0.0, 1.0 - jnp.abs(scaled - (j - (knots - 1) / 2.0)))
                * curve_ref[j : j + 1, :]
                for j in range(knots)
            ]
        )
        usable = (place + k < sections).astype(jnp.float32)
        numerator = numerator + usable * (k * distance)
        denominator = denominator + usable * float(k * k)
    thickness = numerator / jnp.maximum(denominator, 1.0)
    depths = [jnp.zeros((1, tiles), jnp.float32)]
    for s in range(sections - 1):
        depths.append(depths[-1] + thickness[s : s + 1])
    target = depths[-1] * fraction_ref[...]
    bracket = tree_sum(
        [(depths[s] <= target).astype(jnp.int32) for s in range(1, sections)]
    )
    bracket = jnp.minimum(bracket, sections - 2)
    here = [bracket == s for s in range(sections - 1)]
    lower = tree_sum([jnp.where(h, depths[s], 0.0) for s, h in enumerate(here)])
    upper = tree_sum([jnp.where(h, depths[s + 1], 0.0) for s, h in enumerate(here)])
    lifted = bracket.astype(jnp.float32) + (target - lower) / (upper - lower)
    beyond = lifted - bracket.astype(jnp.float32)
    pair = jnp.concatenate(
        [1.0 - jnp.abs(beyond), jnp.maximum(0.0, 1.0 - jnp.abs(beyond - 1.0))], axis=0
    )
    used = lax.broadcasted_iota(jnp.int32, pair.shape, 1) % 4 == 0
    spread_ref[...] = jnp.dot(
        jnp.where(used, jnp.maximum(0.0, pair), 0.0).astype(jnp.bfloat16),
        to_pixels_ref[...],
        preferred_element_type=jnp.float32,
    )
    first = lax.broadcasted_iota(jnp.int32, (rows, LANES), 1) < TILE

    def to_hbm(j):
        some = pl.ds(2 * j, 2)
        return pltpu.make_async_copy(
            made_ref.at[some], out_ref.at[some], out_sems.at[j]
        )

    for j in range(outputs):
        made = []
        for g in range(cols // LANES):
            lanes = pl.ds(g * LANES, LANES)
            ahead = x_ref[pl.ds(bracket[j, lane_of_tile(2 * g)], 2), :, lanes]
            behind = x_ref[pl.ds(bracket[j, lane_of_tile(2 * g + 1)], 2), :, lanes]
            near = jnp.where(first, ahead[0], behind[0])
            far = jnp.where(first, ahead[1], behind[1])
            made.append(
                (
                    spread_ref[j : j + 1, lanes] * near.astype(jnp.float32)
                    + spread_ref[outputs + j : outputs + j + 1, lanes]
                    * far.astype(jnp.float32)
                ).astype(jnp.bfloat16)
            )
        for g, values in enumerate(made):
            made_ref[j, :, g * LANES : (g + 1) * LANES] = values
        if j % 2:
            to_hbm(j // 2).start()
    for j in range(outputs // 2):
        to_hbm(j).wait()


def per_device(sections, calibration_knots, target_offset, target_step):
    section_total = lax.axis_size("sec")
    position = lax.axis_index("sec")
    row_total, cols = sections.shape[1:]
    rows_local = row_total // section_total
    sharers = TILE // rows_local
    tiles = cols // TILE
    if rows_local % 16 or section_total != 16 or tiles * 4 != LANES or sharers > 16:
        return plain_per_device(
            sections, calibration_knots, target_offset, target_step
        )
    blocks = sections.reshape(section_total, rows_local, cols)
    pencils = lax.all_to_all(blocks, "sec", split_axis=0, concat_axis=0, tiled=True)
    height = 8 * (AHEAD + 2) // 2
    vmem = pl.BlockSpec(memory_space=pltpu.VMEM)
    smem = pl.BlockSpec(memory_space=pltpu.SMEM)
    pixels = section_total * rows_local * cols
    tile_row = (position * rows_local // TILE).astype(jnp.int32).reshape(1)
    pairing, to_pixels, fraction, curve = pl.pallas_call(
        tables_kernel,
        out_shape=[
            jax.ShapeDtypeStruct((2 * LANES, LANES), jnp.bfloat16),
            jax.ShapeDtypeStruct((LANES, cols), jnp.bfloat16),
            jax.ShapeDtypeStruct((section_total, LANES), jnp.float32),
            jax.ShapeDtypeStruct((calibration_knots.shape[0], LANES), jnp.float32),
        ],
        in_specs=[smem, smem, vmem, vmem],
        out_specs=[vmem] * 4,
        compiler_params=pltpu.CompilerParams(vmem_limit_bytes=4 * 2**20),
        cost_estimate=pl.CostEstimate(
            flops=2**20, bytes_accessed=2**20, transcendentals=0
        ),
    )(tile_row, calibration_knots, target_offset, target_step)
    partial_sums = pl.pallas_call(
        sums_kernel,
        out_shape=jax.ShapeDtypeStruct((height, LANES), jnp.float32),
        in_specs=[vmem] * 2,
        out_specs=vmem,
        scratch_shapes=[
            pltpu.VMEM(
                (cols // 2 // LANES, section_total * 17, LANES), jnp.float32
            ),
            pltpu.VMEM(
                (cols // 2 // LANES, rows_local // 2, section_total + 8, LANES),
                jnp.float32,
            ),
        ],
        compiler_params=pltpu.CompilerParams(vmem_limit_bytes=16 * 2**20),
        cost_estimate=pl.CostEstimate(
            flops=pixels * 8, bytes_accessed=pixels * 2, transcendentals=0
        ),
    )(pencils, pairing)
    all_sums = [partial_sums]
    for other in range(1, sharers):
        all_sums.append(
            lax.ppermute(
                partial_sums, "sec", [(i, i ^ other) for i in range(section_total)]
            )
        )
    return pl.pallas_call(
        resample_kernel,
        out_shape=jax.ShapeDtypeStruct(pencils.shape, jnp.bfloat16),
        in_specs=[vmem] * (sharers + 4),
        out_specs=pl.BlockSpec(memory_space=pl.ANY),
        scratch_shapes=[
            pltpu.VMEM((2 * section_total, cols), jnp.float32),
            pltpu.VMEM(pencils.shape, jnp.bfloat16),
            pltpu.SemaphoreType.DMA((section_total // 2,)),
        ],
        compiler_params=pltpu.CompilerParams(vmem_limit_bytes=16 * 2**20),
        cost_estimate=pl.CostEstimate(
            flops=pixels * 2 * section_total, bytes_accessed=pixels * 4, transcendentals=0
        ),
    )(fraction, curve, to_pixels, *all_sums, pencils)


def solution(mesh):
    return jax.shard_map(
        per_device,
        mesh=mesh,
        in_specs=(P("sec", None, "tile"), P(), P(None, "tile"), P(None, "tile")),
        out_specs=P(None, "sec", "tile"),
        check_vma=False,
    )
```

```python
import functools

import jax
import jax.numpy as jnp
from jax import lax
from jax.experimental import pallas as pl
from jax.experimental.pallas import tpu as pltpu
from jax.sharding import PartitionSpec as P

TILE = 64
AHEAD = 4
LANES = 128
EPSILON = 1e-06


def from_behind(value, axis, steps):
    count = lax.axis_size(axis)
    first, last = (max(0, -steps), min(count, count - steps))
    return lax.ppermute(value, axis, [(source, source + steps) for source in range(first, last)])


def shrink(pixels):
    leading = pixels.shape[:-2]
    row_total = pixels.shape[-2]
    col_total = pixels.shape[-1]
    blocks = pixels.astype(jnp.float32).reshape(leading + (row_total // 2, 2, col_total // 2, 2))
    return jnp.mean(blocks, axis=(-3, -1)).astype(jnp.bfloat16)


def moments(current, following, row_group, half_tile):
    leading = current.shape[:-2]
    tiled_shape = leading + (
        current.shape[-2] // row_group,
        row_group,
        current.shape[-1] // half_tile,
        half_tile,
    )
    first_tile = current.astype(jnp.float32).reshape(tiled_shape)
    second_tile = following.astype(jnp.float32).reshape(tiled_shape)

    def tile_total(values):
        return jnp.sum(values, axis=(-3, -1))

    return (
        tile_total(first_tile),
        tile_total(second_tile),
        tile_total(first_tile * first_tile),
        tile_total(second_tile * second_tile),
        tile_total(first_tile * second_tile),
    )


def correlate(moment_sums, samples):
    sum_first, sum_second, sum_ff, sum_ss, sum_fs = moment_sums
    mean_first = sum_first / samples
    mean_second = sum_second / samples
    covariance = sum_fs / samples - mean_first * mean_second
    var_first = sum_ff / samples - mean_first * mean_first
    var_second = sum_ss / samples - mean_second * mean_second
    return covariance / jnp.sqrt(var_first * var_second + EPSILON)


def calibrate(correlation, knot_values):
    knot_total = knot_values.shape[0]
    knot_grid = -1.0 + jnp.arange(knot_total, dtype=jnp.float32) * (2.0 / (knot_total - 1))
    hat_weights = jnp.maximum(
        0.0, 1.0 - jnp.abs(correlation[..., None] - knot_grid) * ((knot_total - 1) / 2.0)
    )
    return jnp.sum(hat_weights * (knot_values.astype(jnp.float32) / 1000.0), axis=-1)


def exclusive_last(values):
    running = jnp.cumsum(values, axis=-1)
    return jnp.concatenate(
        [jnp.zeros(values.shape[:-1] + (1,), jnp.float32), running[..., :-1]], axis=-1
    )


def resample_weights(depths, offsets, strides, outputs):
    section_total = depths.shape[-1]
    grid_index = jnp.arange(outputs, dtype=jnp.int32)
    fraction = (offsets[..., None] + grid_index * strides[..., None]).astype(jnp.float32) / (
        64.0 * outputs
    )
    target = depths[..., -1:] * fraction
    bracket = jnp.sum((depths[..., None, 1:] <= target[..., None]).astype(jnp.int32), axis=-1)
    bracket = jnp.minimum(bracket, section_total - 2)
    section_places = jnp.arange(section_total, dtype=jnp.int32)
    lower_depth = jnp.sum(
        jnp.where(section_places == bracket[..., None], depths[..., None, :], 0.0), axis=-1
    )
    upper_depth = jnp.sum(
        jnp.where(section_places == bracket[..., None] + 1, depths[..., None, :], 0.0), axis=-1
    )
    lifted = bracket.astype(jnp.float32) + (target - lower_depth) / (upper_depth - lower_depth)
    spread = jnp.abs(lifted[..., None] - section_places.astype(jnp.float32))
    return jnp.maximum(0.0, 1.0 - spread).astype(jnp.bfloat16)


def plain_per_device(sections, calibration_knots, target_offset, target_step):
    section_total = lax.axis_size("sec")
    position = lax.axis_index("sec")
    half_tile = TILE // 2
    samples = float(half_tile * half_tile)
    row_total = sections.shape[1]
    rows_local = row_total // section_total
    tile_rows = row_total // TILE
    tiles_wide = sections.shape[2] // TILE
    tile_row = position * rows_local // TILE
    pencils = lax.all_to_all(sections, "sec", split_axis=1, concat_axis=0, tiled=True)
    reduced = shrink(sections[0])
    numerator = jnp.zeros((tile_rows, tiles_wide), jnp.float32)
    denominator = jnp.zeros((), jnp.float32)
    for spacing in range(1, AHEAD + 1):
        forward = from_behind(reduced, "sec", -spacing)
        correlation = correlate(moments(reduced, forward, half_tile, half_tile), samples)
        usable = (position + spacing < section_total).astype(jnp.float32)
        numerator = numerator + usable * (spacing * calibrate(correlation, calibration_knots))
        denominator = denominator + usable * float(spacing * spacing)
    thickness = numerator / jnp.maximum(denominator, 1.0)
    spread_rows = jnp.repeat(thickness, TILE, axis=0)[None]
    carried_maps = lax.all_to_all(spread_rows, "sec", split_axis=1, concat_axis=0, tiled=True)
    column_maps = jnp.transpose(carried_maps[:, 0, :])
    depths = exclusive_last(column_maps)
    offsets_row = lax.dynamic_index_in_dim(target_offset, tile_row, 0, keepdims=False)
    strides_row = lax.dynamic_index_in_dim(target_step, tile_row, 0, keepdims=False)
    weights = resample_weights(depths, offsets_row, strides_row, section_total)
    pencil_tiles = pencils.reshape(section_total, rows_local, tiles_wide, TILE)
    resampled = jnp.einsum(
        "tjs,srtc->jrtc", weights, pencil_tiles, preferred_element_type=jnp.float32
    )
    return resampled.reshape(section_total, rows_local, sections.shape[2]).astype(jnp.bfloat16)


def one_hot(shape, row_of, col_of):
    rows = lax.broadcasted_iota(jnp.int32, shape, 0)
    cols = lax.broadcasted_iota(jnp.int32, shape, 1)
    return (row_of(rows) == col_of(cols)).astype(jnp.float32).astype(jnp.bfloat16)


def shift_up(values, steps):
    if steps == 0:
        return values
    return jnp.concatenate([values[steps:], jnp.zeros_like(values[:steps])], axis=0)


def tile_of_lane(lanes):
    group = (lanes // 16) % 2 + 2 * ((lanes // 8) % 2) + 4 * ((lanes // 4) % 2)
    return lanes // 32 + 4 * group


def lane_of_tile(tile):
    group = tile // 4
    return 32 * (tile % 4) + 16 * (group % 2) + 8 * (group // 2 % 2) + 4 * (group // 4)


def tables_kernel(
    tile_row_ref,
    knots_ref,
    offset_ref,
    step_ref,
    pairing_ref,
    to_pixels_ref,
    fraction_ref,
    curve_ref,
):
    pairing_ref[...] = 0.25 * one_hot(pairing_ref.shape, lambda r: r // 2, lambda c: c)
    to_pixels_ref[...] = one_hot(
        to_pixels_ref.shape,
        lambda r: jnp.where(r % 4 == 0, tile_of_lane(r), -1),
        lambda c: c // TILE,
    )
    outputs = fraction_ref.shape[0]
    row = tile_row_ref[0]
    to_lanes = one_hot(
        (offset_ref.shape[1], LANES), lambda r: r, lambda c: tile_of_lane(c)
    )

    def spread(ref):
        values = jnp.broadcast_to(ref[pl.ds(row, 1), :], (16, ref.shape[1]))
        return jnp.dot(
            values.astype(jnp.float32).astype(jnp.bfloat16),
            to_lanes,
            preferred_element_type=jnp.float32,
        )[:1]

    index = lax.broadcasted_iota(jnp.int32, fraction_ref.shape, 0).astype(jnp.float32)
    fraction_ref[...] = (spread(offset_ref) + index * spread(step_ref)) / (
        64.0 * outputs
    )
    for j in range(curve_ref.shape[0]):
        curve_ref[pl.ds(j, 1), :] = jnp.full(
            (1, curve_ref.shape[1]), knots_ref[j].astype(jnp.float32) / 1000.0
        )


def fold(first, second, width, lanes):
    return jnp.where(
        (lanes // width) % 2 == 0,
        first + pltpu.roll(first, LANES - width, 1),
        second + pltpu.roll(second, width, 1),
    )


def sums_kernel(x_ref, pairing_ref, sums_ref, pairs_ref, reduced_ref):
    sections, rows, cols = x_ref.shape
    groups = cols // 2 // LANES
    pairing = pairing_ref[...]
    for g in range(groups):
        wide = x_ref[:, :, 2 * LANES * g : 2 * LANES * (g + 1)]
        pairs = jnp.dot(
            wide.reshape(sections * rows, 2 * LANES),
            pairing,
            preferred_element_type=jnp.float32,
        )
        for s in range(sections):
            pairs_ref[g, pl.ds(17 * s, rows), :] = pairs[rows * s : rows * (s + 1)]
    lanes = lax.broadcasted_iota(jnp.int32, (sections, LANES), 1)
    waiting = {}
    reduced_ref[:, :, sections:, :] = jnp.zeros(
        reduced_ref.shape[:2] + (8, LANES), jnp.float32
    )
    for g in range(groups):
        total = [jnp.zeros((sections, LANES), jnp.float32)] * (AHEAD + 2)
        for r in range(rows // 2):
            upper = pairs_ref[g, pl.ds(2 * r, sections, stride=17), :]
            lower = pairs_ref[g, pl.ds(2 * r + 1, sections, stride=17), :]
            reduced = (upper + lower).astype(jnp.bfloat16).astype(jnp.float32)
            reduced_ref[g, r, :sections] = reduced
            total[0] = total[0] + reduced
            total[1] = total[1] + reduced * reduced
            for k in range(1, AHEAD + 1):
                total[k + 1] = total[k + 1] + reduced * reduced_ref[g, r, k : k + sections]
        width = 16
        while (g * width // 16) % 2 == 1 and width >= 4:
            total = [fold(a, b, width, lanes) for a, b in zip(waiting.pop(width), total)]
            width //= 2
        waiting[width] = total
    total = waiting.pop(2)
    for v in range((AHEAD + 2) // 2):
        pair = fold(total[2 * v], total[2 * v + 1], 2, lanes)
        sums_ref[8 * v : 8 * v + 8] = fold(pair[:8], pair[8:], 1, lanes[:8])


def tree_sum(values):
    while len(values) > 1:
        rest = values[len(values) // 2 * 2 :]
        values = [x + y for x, y in zip(values[::2], values[1::2])] + rest
    return values[0]


def resample_kernel(fraction_ref, curve_ref, to_pixels_ref, *refs):
    *sums_refs, x_ref, out_ref, spread_ref, made_ref, out_sems = refs
    sections, rows, cols = x_ref.shape
    outputs = out_ref.shape[0]
    tiles = LANES
    samples = float((TILE // 2) ** 2)
    packed = sums_refs[0][...]
    for ref in sums_refs[1:]:
        packed = packed + ref[...]

    def unpack(q, half):
        part = packed[8 * (q // 2) : 8 * (q // 2) + 8]
        b = 2 * (q % 2) + half
        return pltpu.roll(part, LANES - b, 1) if b else part

    quantity = [
        jnp.concatenate([unpack(q, 0), unpack(q, 1)], axis=0) for q in range(AHEAD + 2)
    ]
    mean = quantity[0] / samples
    variance = quantity[1] / samples - mean * mean
    place = lax.broadcasted_iota(jnp.int32, (sections, tiles), 0)
    numerator = jnp.zeros((sections, tiles), jnp.float32)
    denominator = jnp.zeros((sections, tiles), jnp.float32)
    knots = curve_ref.shape[0]
    for k in range(1, AHEAD + 1):
        covariance = quantity[k + 1] / samples - mean * shift_up(mean, k)
        correlation = covariance / jnp.sqrt(variance * shift_up(variance, k) + EPSILON)
        scaled = correlation * ((knots - 1) / 2.0)
        distance = tree_sum(
            [
                jnp.maximum(0.0, 1.0 - jnp.abs(scaled - (j - (knots - 1) / 2.0)))
                * curve_ref[j : j + 1, :]
                for j in range(knots)
            ]
        )
        usable = (place + k < sections).astype(jnp.float32)
        numerator = numerator + usable * (k * distance)
        denominator = denominator + usable * float(k * k)
    thickness = numerator / jnp.maximum(denominator, 1.0)
    depths = [jnp.zeros((1, tiles), jnp.float32)]
    for s in range(sections - 1):
        depths.append(depths[-1] + thickness[s : s + 1])
    target = depths[-1] * fraction_ref[...]
    bracket = tree_sum(
        [(depths[s] <= target).astype(jnp.int32) for s in range(1, sections)]
    )
    bracket = jnp.minimum(bracket, sections - 2)
    here = [bracket == s for s in range(sections - 1)]
    lower = tree_sum([jnp.where(h, depths[s], 0.0) for s, h in enumerate(here)])
    upper = tree_sum([jnp.where(h, depths[s + 1], 0.0) for s, h in enumerate(here)])
    lifted = bracket.astype(jnp.float32) + (target - lower) / (upper - lower)
    beyond = lifted - bracket.astype(jnp.float32)
    pair = jnp.concatenate(
        [1.0 - jnp.abs(beyond), jnp.maximum(0.0, 1.0 - jnp.abs(beyond - 1.0))], axis=0
    )
    used = lax.broadcasted_iota(jnp.int32, pair.shape, 1) % 4 == 0
    spread_ref[...] = jnp.dot(
        jnp.where(used, jnp.maximum(0.0, pair), 0.0).astype(jnp.bfloat16),
        to_pixels_ref[...],
        preferred_element_type=jnp.float32,
    )
    first = lax.broadcasted_iota(jnp.int32, (rows, LANES), 1) < TILE

    def to_hbm(j):
        some = pl.ds(2 * j, 2)
        return pltpu.make_async_copy(
            made_ref.at[some], out_ref.at[some], out_sems.at[j]
        )

    for j in range(outputs):
        made = []
        for g in range(cols // LANES):
            lanes = pl.ds(g * LANES, LANES)
            ahead = x_ref[pl.ds(bracket[j, lane_of_tile(2 * g)], 2), :, lanes]
            behind = x_ref[pl.ds(bracket[j, lane_of_tile(2 * g + 1)], 2), :, lanes]
            near = jnp.where(first, ahead[0], behind[0])
            far = jnp.where(first, ahead[1], behind[1])
            made.append(
                (
                    spread_ref[j : j + 1, lanes] * near.astype(jnp.float32)
                    + spread_ref[outputs + j : outputs + j + 1, lanes]
                    * far.astype(jnp.float32)
                ).astype(jnp.bfloat16)
            )
        for g, values in enumerate(made):
            made_ref[j, :, g * LANES : (g + 1) * LANES] = values
        if j % 2:
            to_hbm(j // 2).start()
    for j in range(outputs // 2):
        to_hbm(j).wait()


def per_device(sections, calibration_knots, target_offset, target_step):
    section_total = lax.axis_size("sec")
    position = lax.axis_index("sec")
    row_total, cols = sections.shape[1:]
    rows_local = row_total // section_total
    sharers = TILE // rows_local
    tiles = cols // TILE
    if rows_local % 16 or section_total != 16 or tiles * 4 != LANES or sharers > 16:
        return plain_per_device(
            sections, calibration_knots, target_offset, target_step
        )
    blocks = sections.reshape(section_total, rows_local, cols)
    pencils = lax.all_to_all(blocks, "sec", split_axis=0, concat_axis=0, tiled=True)
    height = 8 * (AHEAD + 2) // 2
    vmem = pl.BlockSpec(memory_space=pltpu.VMEM)
    smem = pl.BlockSpec(memory_space=pltpu.SMEM)
    pixels = section_total * rows_local * cols
    tile_row = (position * rows_local // TILE).astype(jnp.int32).reshape(1)
    pairing, to_pixels, fraction, curve = pl.pallas_call(
        tables_kernel,
        out_shape=[
            jax.ShapeDtypeStruct((2 * LANES, LANES), jnp.bfloat16),
            jax.ShapeDtypeStruct((LANES, cols), jnp.bfloat16),
            jax.ShapeDtypeStruct((section_total, LANES), jnp.float32),
            jax.ShapeDtypeStruct((calibration_knots.shape[0], LANES), jnp.float32),
        ],
        in_specs=[smem, smem, vmem, vmem],
        out_specs=[vmem] * 4,
        compiler_params=pltpu.CompilerParams(vmem_limit_bytes=4 * 2**20),
        cost_estimate=pl.CostEstimate(
            flops=2**20, bytes_accessed=2**20, transcendentals=0
        ),
    )(tile_row, calibration_knots, target_offset, target_step)
    partial_sums = pl.pallas_call(
        sums_kernel,
        out_shape=jax.ShapeDtypeStruct((height, LANES), jnp.float32),
        in_specs=[vmem] * 2,
        out_specs=vmem,
        scratch_shapes=[
            pltpu.VMEM(
                (cols // 2 // LANES, section_total * 17, LANES), jnp.float32
            ),
            pltpu.VMEM(
                (cols // 2 // LANES, rows_local // 2, section_total + 8, LANES),
                jnp.float32,
            ),
        ],
        compiler_params=pltpu.CompilerParams(vmem_limit_bytes=16 * 2**20),
        cost_estimate=pl.CostEstimate(
            flops=pixels * 8, bytes_accessed=pixels * 2, transcendentals=0
        ),
    )(pencils, pairing)
    all_sums = [partial_sums]
    for other in range(1, sharers):
        all_sums.append(
            lax.ppermute(
                partial_sums, "sec", [(i, i ^ other) for i in range(section_total)]
            )
        )
    return pl.pallas_call(
        resample_kernel,
        out_shape=jax.ShapeDtypeStruct(pencils.shape, jnp.bfloat16),
        in_specs=[vmem] * (sharers + 4),
        out_specs=pl.BlockSpec(memory_space=pl.ANY),
        scratch_shapes=[
            pltpu.VMEM((2 * section_total, cols), jnp.float32),
            pltpu.VMEM(pencils.shape, jnp.bfloat16),
            pltpu.SemaphoreType.DMA((section_total // 2,)),
        ],
        compiler_params=pltpu.CompilerParams(vmem_limit_bytes=16 * 2**20),
        cost_estimate=pl.CostEstimate(
            flops=pixels * 2 * section_total, bytes_accessed=pixels * 4, transcendentals=0
        ),
    )(fraction, curve, to_pixels, *all_sums, pencils)


def solution(mesh):
    return jax.shard_map(
        per_device,
        mesh=mesh,
        in_specs=(P("sec", None, "tile"), P(), P(None, "tile"), P(None, "tile")),
        out_specs=P(None, "sec", "tile"),
        check_vma=False,
    )
```
